512 devices in a mesh: blk: 16 (over z_hi, x, core), group: 32 (over y, z_lo).
Axes of the slice: x: 4, y: 8, z: 8 (z_hi: 2, z_lo: 4; z = z_hi * 4 + z_lo), core: 2. Of those that a mesh axis runs over, the one named last changes fastest.
Arguments:
- images: bfloat16 [196608, 768], P(('blk', 'group')), may hold values from -8 to 8
- texts: bfloat16 [196608, 768], P(('blk', 'group')), may hold values from -8 to 8
- logit_scale: float32 [1], replicated, may hold values from 5 to 12
- logit_bias: float32 [1], replicated, may hold values from -3 to -1
Outputs:
- image_grad: float32 [196608, 768], P(('blk', 'group'))
- text_grad: float32 [196608, 768], P(('blk', 'group'))
The draws below stay inside these ranges and needn't reach their ends.
All inputs are finite; a program needn't handle non-finite values.
Results may differ from the reference program's by a relative error of at most 0.0041.
Values may be sent and summed in bfloat16 or wider, within the bound.
No kernel may reach another device: no remote copies, remote signals or barrier semaphores. Data moves between devices by JAX's collectives and lax.ppermute only.
A program may use at most 64 MiB of HBM per device.

```python
import math
import jax
import jax.numpy as jnp
from jax import lax

D = 768
ROWS = 384
STEPS = 4
NROWS = 196608
N_BLK = 16
N_GROUP = 32


def scaled_rows(key, values, row_top):
    key_rows, key_cols = jax.random.split(key)
    row_scale = jnp.exp(jax.random.uniform(key_rows, (NROWS, 1), jnp.float32) * math.log(row_top))
    col_scale = jnp.exp(jax.random.uniform(key_cols, (1, D), jnp.float32) * math.log(10.0))
    return values * row_scale * col_scale * 0.02


def draw_embeddings(key):
    key_values, key_scales = jax.random.split(key, 2)
    values = jnp.clip(jax.random.normal(key_values, (NROWS, D), jnp.float32), -4.0, 4.0)
    drawn = scaled_rows(key_scales, values, 10.0)
    return jnp.clip(drawn, -8.0, 8.0).astype(jnp.bfloat16)


def draw_images(key, part):
    key = jax.random.fold_in(key, 11)
    return draw_embeddings(key)


def draw_texts(key, part):
    key = jax.random.fold_in(key, 12)
    return draw_embeddings(key)


def setup_inputs(seed: int = 0) -> dict:
    arg_keys = jax.random.split(jax.random.key(seed), 5)
    images = draw_images(jax.random.fold_in(arg_keys[4], 71), 0)
    texts = draw_texts(jax.random.fold_in(arg_keys[4], 71), 0)
    logit_scale = jnp.clip(jax.random.uniform(arg_keys[2], (1,), jnp.float32, 5.0, 12.0), 5.0, 12.0)
    logit_bias = jnp.clip(jax.random.uniform(arg_keys[3], (1,), jnp.float32, -3.0, -1.0), -3.0, -1.0)
    return dict(images=images, texts=texts, logit_scale=logit_scale, logit_bias=logit_bias)


epsilon = 1e-06

def normalize(values):
    full = values.astype(jnp.float32)
    inverse = lax.rsqrt(lax.optimization_barrier(jnp.sum(full * full, axis=-1, keepdims=True)) + epsilon)
    return (full * inverse, inverse)

def project(grad, unit, inverse):
    return (grad - unit * lax.optimization_barrier(jnp.sum(unit * grad, axis=-1, keepdims=True))) * inverse

def partner_flip(blocks):
    shaped = blocks.reshape(N_BLK, N_GROUP // 2, 2, ROWS, D)
    return shaped[:, :, ::-1].reshape(N_BLK, N_GROUP, ROWS, D)

def reference(images, texts, logit_scale, logit_bias):
    scale_value = logit_scale[0]
    bias_value = logit_bias[0]
    image_unit, image_inv = normalize(images)
    text_unit, text_inv = normalize(texts)
    image_hat = lax.optimization_barrier(image_unit.astype(jnp.bfloat16)).astype(jnp.float32)
    text_hat = lax.optimization_barrier(text_unit.astype(jnp.bfloat16)).astype(jnp.float32)
    image_blocks = image_hat.reshape(N_BLK, N_GROUP, ROWS, D)
    text_blocks = text_hat.reshape(N_BLK, N_GROUP, ROWS, D)
    diagonal_mask = jnp.eye(ROWS, dtype=bool)
    image_sum = jnp.zeros((N_BLK, N_GROUP, ROWS, D), jnp.float32)
    text_sum = jnp.zeros((N_BLK, N_GROUP, ROWS, D), jnp.float32)
    for step in range(STEPS):
        for partner_side in (0, 1):
            source = text_blocks if partner_side == 0 else partner_flip(text_blocks)
            visiting = jnp.roll(source, step, axis=0)
            logits = scale_value * jnp.einsum('bgid,bgjd->bgij', image_blocks, visiting) + bias_value
            if step == 0 and partner_side == 0:
                signs = jnp.where(diagonal_mask, 1.0, -1.0).astype(jnp.float32)
            else:
                signs = -jnp.ones((ROWS, ROWS), jnp.float32)
            slopes = (scale_value * signs * (jax.nn.sigmoid(signs * logits) - 1.0)).astype(jnp.bfloat16)
            slopes = lax.optimization_barrier(slopes).astype(jnp.float32)
            image_sum = image_sum + jnp.einsum('bgij,bgjd->bgid', slopes, visiting)
            text_term = jnp.einsum('bgij,bgid->bgjd', slopes, image_blocks)
            text_term = jnp.roll(text_term, -step, axis=0)
            if partner_side == 1:
                text_term = partner_flip(text_term)
            text_sum = text_sum + text_term
    image_grad = project(image_sum.reshape(NROWS, D), image_unit, image_inv)
    text_grad = project(text_sum.reshape(NROWS, D), text_unit, text_inv)
    return (image_grad, text_grad)
```

```python
import functools

import jax
import jax.numpy as jnp
from jax import lax
from jax.experimental import pallas as pl
from jax.experimental.pallas import tpu as pltpu
from jax.sharding import PartitionSpec as P

AXES = ("blk", "group")
EPSILON = 1e-06
VMEM_LIMIT = 48 * 1024 * 1024

VMEM = pl.BlockSpec(memory_space=pltpu.VMEM)
SMEM = pl.BlockSpec(memory_space=pltpu.SMEM)
PARAMS = pltpu.CompilerParams(vmem_limit_bytes=VMEM_LIMIT)


def shift_pairs(size, by):
    return [(b, (b + by) % size) for b in range(size)]


def core_pairs(size):
    return [(b, b ^ 1) for b in range(size)]


def odd_pairs(size, by):
    return [(b, (b + by) % size if b % 2 else b) for b in range(size)]


def partner_pairs(size):
    return [(g, g ^ 1) for g in range(size)]


def normalize(values):
    full = values.astype(jnp.float32)
    inverse = lax.rsqrt(jnp.sum(full * full, axis=-1, keepdims=True) + EPSILON)
    return full * inverse, inverse


def hat(values):
    return normalize(values)[0].astype(jnp.bfloat16)


def dot(left, right, left_dim, right_dim):
    return lax.dot_general(
        left, right, (((left_dim,), (right_dim,)), ((), ())), preferred_element_type=jnp.float32
    )


def slopes_of(image_hat, text_hat, scale, bias, same=None):
    chance = jax.nn.sigmoid(scale * dot(image_hat, text_hat, 1, 1) + bias)
    if same is not None:
        chance = chance - same
    return (scale * chance).astype(jnp.bfloat16)


def own_kernel(scale_ref, bias_ref, text_ref, image_ref, partner_ref, own_ref, other_ref, text_grad_ref):
    scale, bias = scale_ref[0], bias_ref[0]
    text_hat = hat(text_ref[...])
    rows = text_hat.shape[0]
    same = (
        lax.broadcasted_iota(jnp.int32, (rows, rows), 0)
        == lax.broadcasted_iota(jnp.int32, (rows, rows), 1)
    ).astype(jnp.float32)
    image_hat = hat(image_ref[...])
    slopes = slopes_of(image_hat, text_hat, scale, bias, same)
    own_ref[...] = dot(slopes, text_hat, 1, 0)
    text_grad_ref[...] = dot(slopes, image_hat, 0, 0)
    image_hat = hat(partner_ref[...])
    slopes = slopes_of(image_hat, text_hat, scale, bias)
    other_ref[...] = dot(slopes, text_hat, 1, 0)
    text_grad_ref[...] += dot(slopes, image_hat, 0, 0)


def rest_kernel(
    scale_ref, bias_ref, near_ref, far_ref, i0, i1, i2, i3, own_ref, other_ref,
    own_out, other_out, cross_out, near_grad_out, far_grad_out, images, grads, text_sum,
):
    scale, bias = scale_ref[0], bias_ref[0]
    for slot, ref in enumerate((i0, i1, i2, i3)):
        images[slot] = hat(ref[...])
    grads[0] = own_ref[...]
    grads[1] = other_ref[...]
    grads[2] = jnp.zeros_like(own_ref)
    grads[3] = jnp.zeros_like(own_ref)

    def against(text_ref, first, out_ref):
        text_hat = hat(text_ref[...])
        text_sum[...] = jnp.zeros_like(text_sum)

        def step(slot, carry):
            image_hat = images[slot]
            slopes = slopes_of(image_hat, text_hat, scale, bias)
            grads[slot] += dot(slopes, text_hat, 1, 0)
            text_sum[...] += dot(slopes, image_hat, 0, 0)
            return carry

        lax.fori_loop(first, 4, step, 0)
        out_ref[...] = text_sum[...].astype(out_ref.dtype)

    against(near_ref, 0, near_grad_out)
    against(far_ref, 2, far_grad_out)
    own_out[...] = grads[0]
    other_out[...] = grads[1]
    cross_out[0] = grads[2].astype(cross_out.dtype)
    cross_out[1] = grads[3].astype(cross_out.dtype)


def final_kernel(count, *refs):
    raw_ref, sum_ref = refs[0], refs[1]
    total = sum_ref[...]
    for ref in refs[2 : 2 + count]:
        total = total + ref[...].astype(jnp.float32)
    unit, inverse = normalize(raw_ref[...])
    out_ref = refs[-1]
    out_ref[...] = (total - unit * jnp.sum(unit * total, axis=-1, keepdims=True)) * inverse


def finish(raw, total, *received):
    rows, width = raw.shape
    block = pl.BlockSpec((rows // 3, width), lambda i: (i, 0))
    return pl.pallas_call(
        functools.partial(final_kernel, len(received)),
        grid=(3,),
        in_specs=[block] * (2 + len(received)),
        out_specs=block,
        out_shape=jax.ShapeDtypeStruct(raw.shape, jnp.float32),
        compiler_params=PARAMS,
    )(raw, total, *received)


def on_device(images, texts, logit_scale, logit_bias):
    n_blk = lax.axis_size("blk")
    n_group = lax.axis_size("group")
    rows, width = images.shape
    full = jax.ShapeDtypeStruct((rows, width), jnp.float32)
    half = jax.ShapeDtypeStruct((rows, width), jnp.bfloat16)
    pair = jax.ShapeDtypeStruct((2, rows, width), jnp.bfloat16)

    def along_blk(values, pairs):
        return lax.ppermute(values, "blk", pairs)

    def to_partner(values):
        return lax.ppermute(values, "group", partner_pairs(n_group))

    near = along_blk(texts, shift_pairs(n_blk, 2))
    far = along_blk(texts, odd_pairs(n_blk, 4))
    partner = to_partner(images)
    other = along_blk(images, core_pairs(n_blk))
    other_partner = along_blk(partner, core_pairs(n_blk))

    own_grad, partner_grad, text_grad = pl.pallas_call(
        own_kernel,
        in_specs=[SMEM, SMEM, VMEM, VMEM, VMEM],
        out_specs=[VMEM] * 3,
        out_shape=[full] * 3,
        compiler_params=PARAMS,
    )(logit_scale, logit_bias, texts, images, partner)

    own_grad, partner_grad, cross, near_grad, far_grad = pl.pallas_call(
        rest_kernel,
        in_specs=[SMEM, SMEM] + [VMEM] * 8,
        out_specs=[VMEM] * 5,
        out_shape=[full, full, pair, half, half],
        scratch_shapes=[
            pltpu.VMEM((4, rows, width), jnp.bfloat16),
            pltpu.VMEM((4, rows, width), jnp.float32),
            pltpu.VMEM((rows, width), jnp.float32),
        ],
        compiler_params=PARAMS,
    )(
        logit_scale, logit_bias, near, far, images, partner, other, other_partner,
        own_grad, partner_grad,
    )

    near_back = along_blk(near_grad, shift_pairs(n_blk, -2))
    far_back = along_blk(far_grad, odd_pairs(n_blk, -4))
    cross = along_blk(cross, core_pairs(n_blk))
    partner_total = (partner_grad + cross[1].astype(jnp.float32)).astype(jnp.bfloat16)
    partner_back = to_partner(partner_total)
    image_grad = finish(images, own_grad, cross[0], partner_back)
    text_grad = finish(texts, text_grad, near_back, far_back)
    return image_grad, text_grad


def solution(mesh):
    return jax.shard_map(
        on_device,
        mesh=mesh,
        in_specs=(P(AXES, None), P(AXES, None), P(), P()),
        out_specs=(P(AXES, None), P(AXES, None)),
        check_vma=False,
    )
```

```python
import functools

import jax
import jax.numpy as jnp
from jax import lax
from jax.experimental import pallas as pl
from jax.experimental.pallas import tpu as pltpu
from jax.sharding import PartitionSpec as P

AXES = ("blk", "group")
EPSILON = 1e-06
CHIPS = 4
CHUNKS = 2

SMEM = pl.BlockSpec(memory_space=pltpu.SMEM)
WHOLE = pl.BlockSpec(memory_space=pltpu.VMEM)


def params(mib):
    return pltpu.CompilerParams(vmem_limit_bytes=mib * 1024 * 1024)


def near_to(b, g, size):
    to = (b + 2) % size
    return to, g ^ (to // (2 * CHIPS) != b // (2 * CHIPS))


def far_to(b, g, size):
    if b % 2 == 0:
        return b, g
    to = (b + 4) % size
    return to, g ^ (to // (2 * CHIPS) != b // (2 * CHIPS))


def other_core(b, g, size):
    return b ^ 1, g


def partner(b, g, size):
    return b, g ^ 1


def move(values, where, inverse=False):
    n_blk, n_group = lax.axis_size("blk"), lax.axis_size("group")
    pairs = []
    for b in range(n_blk):
        for g in range(n_group):
            to_b, to_g = where(b, g, n_blk)
            pair = (b * n_group + g, to_b * n_group + to_g)
            pairs.append(pair[::-1] if inverse else pair)
    return lax.ppermute(values, AXES, sorted(pairs))


def normalize(values):
    full = values.astype(jnp.float32)
    inverse = lax.rsqrt(jnp.sum(full * full, axis=-1, keepdims=True) + EPSILON)
    return full * inverse, inverse


def hat(values):
    return normalize(values)[0].astype(jnp.bfloat16)


def dot(left, right, left_dim, right_dim):
    return lax.dot_general(
        left, right, (((left_dim,), (right_dim,)), ((), ())), preferred_element_type=jnp.float32
    )


def slopes_of(text_hat, image_hat, scale, bias, same=None):
    chance = jax.nn.sigmoid(scale * dot(text_hat, image_hat, 1, 1) + bias)
    if same is not None:
        chance = chance - same
    return (scale * chance).astype(jnp.bfloat16)


def own_kernel(scale_ref, bias_ref, text_ref, image_ref, partner_ref, text_grad_ref, slopes_ref, hat_ref):
    scale, bias = scale_ref[0], bias_ref[0]
    text_hat = hat(text_ref[...])
    rows = text_hat.shape[0]
    same = (
        lax.broadcasted_iota(jnp.int32, (rows, rows), 0)
        == lax.broadcasted_iota(jnp.int32, (rows, rows), 1)
    ).astype(jnp.float32)
    image_hat = hat(image_ref[...])
    slopes = slopes_of(text_hat, image_hat, scale, bias, same)
    slopes_ref[0] = slopes
    total = dot(slopes, image_hat, 1, 0)
    image_hat = hat(partner_ref[...])
    slopes = slopes_of(text_hat, image_hat, scale, bias)
    slopes_ref[1] = slopes
    text_grad_ref[...] = total + dot(slopes, image_hat, 1, 0)
    hat_ref[...] = text_hat


def hats_kernel(*refs):
    for slot, ref in enumerate(refs[:-1]):
        refs[-1][slot] = hat(ref[...])


def text_kernel(scale_ref, bias_ref, text_ref, images_ref, text_grad_ref, slopes_ref, hat_ref):
    count, rows, width = images_ref.shape
    text_hat = hat(text_ref[...])
    images = images_ref[...].reshape(count * rows, width)
    slopes = slopes_of(text_hat, images, scale_ref[0], bias_ref[0])
    text_grad_ref[...] = dot(slopes, images, 1, 0).astype(text_grad_ref.dtype)
    for slot in range(count):
        slopes_ref[slot] = slopes[:, slot * rows : (slot + 1) * rows]
    hat_ref[...] = text_hat


def image_kernel(count, *refs):
    total = None
    for slopes_ref, hat_ref in zip(refs[:count], refs[count : 2 * count]):
        term = dot(slopes_ref[0], hat_ref[...], 0, 0)
        total = term if total is None else total + term
    for ref in refs[2 * count : -1]:
        total = total + ref[...].astype(jnp.float32)
    refs[-1][...] = total.astype(refs[-1].dtype)


def final_kernel(parts, *refs):
    raw_ref, out_ref = refs[0], refs[-1]
    total = refs[1][...]
    at = 2
    for count in parts:
        pieces = [ref[...] for ref in refs[at : at + count]]
        at += count
        piece = pieces[0] if count == 1 else jnp.concatenate(pieces, axis=0)
        total = total + piece.astype(jnp.float32)
    unit, inverse = normalize(raw_ref[...])
    out_ref[...] = (total - unit * jnp.sum(unit * total, axis=-1, keepdims=True)) * inverse


def finish(raw, total, *received):
    flat = [piece for pieces in received for piece in pieces]
    return pl.pallas_call(
        functools.partial(final_kernel, [len(pieces) for pieces in received]),
        in_specs=[WHOLE] * (2 + len(flat)),
        out_specs=WHOLE,
        out_shape=jax.ShapeDtypeStruct(raw.shape, jnp.float32),
        compiler_params=params(12),
    )(raw, total, *flat)


def on_device(images, texts, logit_scale, logit_bias):
    rows, width = images.shape
    part = rows // CHUNKS
    bf16 = functools.partial(jax.ShapeDtypeStruct, dtype=jnp.bfloat16)
    full = jax.ShapeDtypeStruct((rows, width), jnp.float32)

    near = [move(texts[i * part : (i + 1) * part], near_to) for i in range(CHUNKS)]
    far = move(texts, far_to)
    partner_images = move(images, partner)
    other_images = move(images, other_core)
    positive = logit_scale[0] > 0

    def swap_cores(values):
        return move(values, other_core)

    other_partner = lax.cond(positive, swap_cores, swap_cores, partner_images)

    text_grad, own_slopes, own_hat = pl.pallas_call(
        own_kernel,
        in_specs=[SMEM, SMEM] + [WHOLE] * 3,
        out_specs=[WHOLE] * 3,
        out_shape=[full, bf16((2, rows, rows)), bf16((rows, width))],
        compiler_params=params(16),
    )(logit_scale, logit_bias, texts, images, partner_images)

    all_hats = pl.pallas_call(
        hats_kernel,
        in_specs=[WHOLE] * 4,
        out_specs=WHOLE,
        out_shape=bf16((4, rows, width)),
        compiler_params=params(12),
    )(images, partner_images, other_images, other_partner)

    def against(text, count):
        size = text.shape[0]
        return pl.pallas_call(
            text_kernel,
            grid=(1,),
            in_specs=[
                SMEM,
                SMEM,
                pl.BlockSpec((size, width), lambda i: (0, 0)),
                pl.BlockSpec((count, rows, width), lambda i: (4 // count - 1, 0, 0)),
            ],
            out_specs=[
                pl.BlockSpec((size, width), lambda i: (0, 0)),
                pl.BlockSpec((count, size, rows), lambda i: (0, 0, 0)),
                pl.BlockSpec((size, width), lambda i: (0, 0)),
            ],
            out_shape=[bf16((size, width)), bf16((count, size, rows)), bf16((size, width))],
            compiler_params=params(20),
        )(logit_scale, logit_bias, text, all_hats)

    far_grad, far_slopes, far_hat = against(far, 2)
    far_back = move(far_grad, far_to, True)
    terms = [against(text, 4) for text in near]
    near_back = [move(grad, near_to, True) for grad, _, _ in terms]

    def image_sum(sources, dtype, *more):
        slopes = [s for s, _, _ in sources]
        hats = [h for _, h, _ in sources]
        slots = [slot for _, _, slot in sources]
        return pl.pallas_call(
            functools.partial(image_kernel, len(sources)),
            grid=(1,),
            in_specs=[
                pl.BlockSpec((1,) + s.shape[1:], lambda i, slot=slot: (slot, 0, 0))
                for s, slot in zip(slopes, slots)
            ]
            + [pl.BlockSpec(a.shape, lambda i: (0, 0)) for a in hats + list(more)],
            out_specs=pl.BlockSpec((rows, width), lambda i: (0, 0)),
            out_shape=jax.ShapeDtypeStruct((rows, width), dtype),
            compiler_params=params(20),
        )(*slopes, *hats, *more)

    def near_terms(slot):
        return [(s, h, slot) for _, s, h in terms]

    cross_partner = image_sum(near_terms(3) + [(far_slopes, far_hat, 1)], jnp.bfloat16)
    cross_own = image_sum(near_terms(2) + [(far_slopes, far_hat, 0)], jnp.bfloat16)

    def exchange(cross_partner, cross_own, near_slopes, near_hats, own_slopes, own_hat):
        cross_partner = move(cross_partner, other_core)
        cross_own = move(cross_own, other_core)
        sources = [(s, h, 1) for s, h in zip(near_slopes + [own_slopes], near_hats + [own_hat])]
        from_partner = move(image_sum(sources, jnp.bfloat16, cross_partner), partner)
        return cross_own, from_partner

    cross_own, from_partner = lax.cond(
        positive,
        exchange,
        exchange,
        cross_partner,
        cross_own,
        [s for _, s, _ in terms],
        [h for _, _, h in terms],
        own_slopes,
        own_hat,
    )
    own_grad = image_sum(near_terms(0) + [(own_slopes, own_hat, 0)], jnp.float32)

    image_grad = finish(images, own_grad, [cross_own], [from_partner])
    text_grad = finish(texts, text_grad, near_back, [far_back])
    return image_grad, text_grad


def solution(mesh):
    return jax.shard_map(
        on_device,
        mesh=mesh,
        in_specs=(P(AXES, None), P(AXES, None), P(), P()),
        out_specs=(P(AXES, None), P(AXES, None)),
        check_vma=False,
    )
```

```python
import functools

import jax
import jax.numpy as jnp
from jax import lax
from jax.experimental import pallas as pl
from jax.experimental.pallas import tpu as pltpu
from jax.sharding import PartitionSpec as P

AXES = ("blk", "group")
EPSILON = 1e-06
CHIPS = 4

SMEM = pl.BlockSpec(memory_space=pltpu.SMEM)
WHOLE = pl.BlockSpec(memory_space=pltpu.VMEM)


def params(mib):
    return pltpu.CompilerParams(vmem_limit_bytes=mib * 1024 * 1024)


def near_to(b, g, size):
    to = (b + 2) % size
    return to, g ^ (to // (2 * CHIPS) != b // (2 * CHIPS))


def crossed(b, to):
    return to // (2 * CHIPS) != b // (2 * CHIPS)


def guest_to(b, g, size):
    if b % 2 == 1:
        return None
    to = (b - 1) % size
    return to, g ^ crossed(b, to)


def guest_partner_to(b, g, size):
    if b % 2 == 1:
        return None
    to = (b - 1) % size
    return to, g ^ 1 ^ crossed(b, to)


def far_to(b, g, size):
    return ((b + 3) % size, g ^ 1) if b % 2 == 1 and b // 2 % CHIPS == CHIPS - 2 else None


def inside(where):
    def to(b, g, size):
        end = where(b, g, size)
        return end if b % 2 == 0 and b // 2 % CHIPS > 0 else None

    return to


def other_core(b, g, size):
    return b ^ 1, g


def partner(b, g, size):
    return b, g ^ 1


def move(values, where, inverse=False):
    n_blk, n_group = lax.axis_size("blk"), lax.axis_size("group")
    pairs = []
    for b in range(n_blk):
        for g in range(n_group):
            to = where(b, g, n_blk)
            if to is not None:
                pair = (b * n_group + g, to[0] * n_group + to[1])
                pairs.append(pair[::-1] if inverse else pair)
    return lax.ppermute(values, AXES, sorted(pairs))


def normalize(values):
    full = values.astype(jnp.float32)
    inverse = lax.rsqrt(jnp.sum(full * full, axis=-1, keepdims=True) + EPSILON)
    return full * inverse, inverse


def hat(values):
    return normalize(values)[0].astype(jnp.bfloat16)


def dot(left, right, left_dim, right_dim):
    return lax.dot_general(
        left, right, (((left_dim,), (right_dim,)), ((), ())), preferred_element_type=jnp.float32
    )


def slopes_of(text_hat, image_hat, scale, bias, same=None):
    chance = jax.nn.sigmoid(scale * dot(text_hat, image_hat, 1, 1) + bias)
    if same is not None:
        chance = chance - same
    return (scale * chance).astype(jnp.bfloat16)


def rows_of(ref):
    count, rows, width = ref.shape
    return ref[...].reshape(count * rows, width)


def is_odd(role):
    return role[0] == 1


def takes_far(role):
    return jnp.logical_and(role[0] == 0, role[1] == 0)


def hats_kernel(image_ref, partner_ref, hats_ref):
    hats_ref[0] = hat(image_ref[...])
    hats_ref[1] = hat(partner_ref[...])


def own_kernel(
    role, scale_ref, bias_ref, text_ref, mine_ref, text_sum_ref, mine_sum_ref, partner_sum_ref,
):
    scale, bias = scale_ref[0], bias_ref[0]
    rows, width = text_ref.shape
    text_hat = hat(text_ref[...])
    same = (
        lax.broadcasted_iota(jnp.int32, (rows, 2 * rows), 0)
        == lax.broadcasted_iota(jnp.int32, (rows, 2 * rows), 1)
    ).astype(jnp.float32)
    images = rows_of(mine_ref)
    slopes = slopes_of(text_hat, images, scale, bias, same)
    text_sum_ref[...] = dot(slopes, images, 1, 0)
    mine_sum_ref[...] = dot(slopes[:, :rows], text_hat, 0, 0)
    partner_sum_ref[...] = dot(slopes[:, rows:], text_hat, 0, 0)


def near_kernel(
    role, scale_ref, bias_ref, text_ref, mine_ref, theirs_ref, guest_ref, guest_partner_ref, far_ref,
    grad_ref, slopes_ref, hat_ref, guest_slopes_ref, back_partner_ref, far_slopes_ref, far_hat_ref,
    images_ref,
):
    scale, bias = scale_ref[0], bias_ref[0]
    rows, width = text_ref.shape
    hat_ref[...] = hat(text_ref[...])
    for slot in range(2):
        images_ref[slot] = mine_ref[slot]
        images_ref[2 + slot] = theirs_ref[slot]

    @pl.when(role[0] == 0)
    def _():
        images = images_ref[:4].reshape(4 * rows, width)
        slopes = slopes_of(hat_ref[...], images, scale, bias)
        slopes_ref[...] = slopes
        grad_ref[...] = dot(slopes, images, 1, 0).astype(grad_ref.dtype)

    @pl.when(role[0] == 1)
    def _():
        images_ref[4] = hat(guest_ref[...])
        images_ref[5] = hat(guest_partner_ref[...])
        images = rows_of(images_ref)
        near_hat = hat_ref[...]
        slopes = slopes_of(near_hat, images, scale, bias)
        grad_ref[...] = dot(slopes, images, 1, 0).astype(grad_ref.dtype)
        slopes_ref[...] = slopes[:, : 4 * rows]
        guest_slopes_ref[...] = slopes[:, 4 * rows : 5 * rows]
        back_partner_ref[...] = dot(slopes[:, 5 * rows :], near_hat, 0, 0).astype(back_partner_ref.dtype)

    @pl.when(takes_far(role))
    def _():
        text_hat = hat(far_ref[...])
        far_hat_ref[...] = text_hat
        far_slopes_ref[...] = slopes_of(text_hat, rows_of(mine_ref), scale, bias)


def theirs_kernel(
    role, scale_ref, bias_ref, slopes_ref, hat_ref, text_ref, theirs_ref, text_sum_ref, guest_slopes_ref,
    cross_ref, text_sum_out, back_ref,
):
    rows, width = text_ref.shape
    near_hat = hat_ref[...]

    @pl.when(role[0] == 0)
    def _():
        text_hat = hat(text_ref[...])
        images = rows_of(theirs_ref)
        own = slopes_of(text_hat, images, scale_ref[0], bias_ref[0])
        text_sum_out[...] = text_sum_ref[...] + dot(own, images, 1, 0)
        for slot in range(2):
            at = slice((2 + slot) * rows, (3 + slot) * rows)
            total = dot(slopes_ref[:, at], hat_ref[...], 0, 0)
            total = total + dot(own[:, slot * rows : (slot + 1) * rows], text_hat, 0, 0)
            cross_ref[slot] = total.astype(cross_ref.dtype)

    @pl.when(role[0] == 1)
    def _():
        text_sum_out[...] = text_sum_ref[...]
        for slot in range(2):
            at = slice((2 + slot) * rows, (3 + slot) * rows)
            cross_ref[slot] = dot(slopes_ref[:, at], hat_ref[...], 0, 0).astype(cross_ref.dtype)
        back_ref[...] = dot(guest_slopes_ref[...], hat_ref[...], 0, 0).astype(back_ref.dtype)


def partner_kernel(role, slopes_ref, hat_ref, far_slopes_ref, far_hat_ref, sum_ref, cross_ref, back_ref, out_ref, total):
    rows = hat_ref.shape[0]
    even = 1.0 - is_odd(role).astype(jnp.float32)
    total[...] = (
        dot(slopes_ref[:, rows : 2 * rows], hat_ref[...], 0, 0)
        + sum_ref[...]
        + cross_ref[0].astype(jnp.float32)
        + even * back_ref[...].astype(jnp.float32)
    )

    @pl.when(takes_far(role))
    def _():
        total[...] += dot(far_slopes_ref[:, rows:], far_hat_ref[...], 0, 0)

    out_ref[...] = total[...].astype(out_ref.dtype)


def mine_kernel(role, slopes_ref, hat_ref, far_slopes_ref, far_hat_ref, sum_ref, cross_ref, out_ref, total):
    rows = hat_ref.shape[0]
    out_ref[...] = (
        dot(slopes_ref[:, :rows], hat_ref[...], 0, 0) + sum_ref[...] + cross_ref[0].astype(jnp.float32)
    )

    @pl.when(takes_far(role))
    def _():
        out_ref[...] += dot(far_slopes_ref[:, :rows], far_hat_ref[...], 0, 0)


def project(raw, total):
    unit, inverse = normalize(raw)
    return (total - unit * jnp.sum(unit * total, axis=-1, keepdims=True)) * inverse


def text_final_kernel(role, texts, text_sum, near_back, role_out, out_ref):
    role_out[0] = role[0]
    out_ref[...] = project(texts[...], text_sum[...] + near_back[...].astype(jnp.float32))


def image_final_kernel(role, images, image_sum, from_partner, back, out_ref):
    even = 1.0 - is_odd(role).astype(jnp.float32)
    total = image_sum[...] + from_partner[...].astype(jnp.float32) + even * back[...].astype(jnp.float32)
    out_ref[...] = project(images[...], total)


def call(kernel, out_shape, *operands, mib=16, scalars=3, scalar_outs=0, scratch=()):
    outs = out_shape if isinstance(out_shape, list) else [out_shape]
    out_specs = [SMEM] * scalar_outs + [WHOLE] * (len(outs) - scalar_outs)
    return pl.pallas_call(
        kernel,
        in_specs=[SMEM] * scalars + [WHOLE] * (len(operands) - scalars),
        out_specs=out_specs if isinstance(out_shape, list) else out_specs[0],
        out_shape=out_shape,
        scratch_shapes=list(scratch),
        compiler_params=params(mib),
    )(*operands)


def on_device(images, texts, logit_scale, logit_bias):
    rows, width = images.shape
    bf16 = functools.partial(jax.ShapeDtypeStruct, dtype=jnp.bfloat16)
    full = jax.ShapeDtypeStruct((rows, width), jnp.float32)
    half = bf16((rows, width))
    half_pair = bf16((2, rows, width))

    index = lax.axis_index("blk")
    role = jnp.stack([index % 2, index // 2 % CHIPS]).astype(jnp.int32)
    scalars = (role, logit_scale, logit_bias)
    positive = logit_scale[0] > 0

    def together(body, *operands):
        return lax.cond(positive, body, body, *operands)

    partner_images = move(images, partner)
    near = move(texts, near_to)
    guest = move(images, guest_to)
    guest_partner = move(images, guest_partner_to)
    far = move(texts, far_to)
    mine = call(hats_kernel, half_pair, images, partner_images, scalars=0)
    theirs = together(lambda values: move(values, other_core), mine)
    text_sum, mine_sum, partner_sum = call(own_kernel, [full, full, full], *scalars, texts, mine)
    near_grad, slopes, near_hat, guest_slopes, back_partner, far_slopes, far_hat = call(
        near_kernel,
        [half, bf16((rows, 4 * rows)), half, bf16((rows, rows)), half, bf16((rows, 2 * rows)), half],
        *scalars, near, mine, theirs, guest, guest_partner, far,
        scratch=[pltpu.VMEM((6, rows, width), jnp.bfloat16)],
        mib=24,
    )
    near_back = move(near_grad, near_to, True)
    back_partner = move(back_partner, inside(guest_to), True)
    cross, text_sum, back = call(
        theirs_kernel,
        [half_pair, full, half],
        *scalars, slopes, near_hat, texts, theirs, text_sum, guest_slopes,
    )

    def sum_with_cross(kernel, slot, dtype, *operands):
        specs = []
        for operand in operands:
            if operand.shape == (2,):
                specs.append(SMEM)
            elif operand.ndim == 3:
                specs.append(pl.BlockSpec((1, rows, width), lambda i: (slot, 0, 0)))
            else:
                specs.append(pl.BlockSpec(operand.shape, lambda i: (0, 0)))
        return pl.pallas_call(
            kernel,
            grid=(1,),
            in_specs=specs,
            out_specs=pl.BlockSpec((rows, width), lambda i: (0, 0)),
            out_shape=jax.ShapeDtypeStruct((rows, width), dtype),
            scratch_shapes=[pltpu.VMEM((rows, width), jnp.float32)],
            compiler_params=params(20),
        )(*operands)

    def across(cross, role, slopes, near_hat, far_slopes, far_hat, partner_sum, back_partner):
        cross = move(cross, other_core)
        return cross, sum_with_cross(
            partner_kernel, 1, jnp.bfloat16,
            role, slopes, near_hat, far_slopes, far_hat, partner_sum, cross, back_partner,
        )

    cross, for_partner = together(
        across, cross, role, slopes, near_hat, far_slopes, far_hat, partner_sum, back_partner
    )
    from_partner = move(for_partner, partner)
    back = together(lambda values: move(values, inside(guest_to), True), back)
    image_sum = sum_with_cross(
        mine_kernel, 0, jnp.float32, role, slopes, near_hat, far_slopes, far_hat, mine_sum, cross
    )
    role, text_grad = call(
        text_final_kernel,
        [jax.ShapeDtypeStruct((2,), jnp.int32), full],
        role, texts, text_sum, near_back,
        scalars=1, scalar_outs=1,
    )
    image_grad = call(image_final_kernel, full, role, images, image_sum, from_partner, back, scalars=1)
    return image_grad, text_grad


def solution(mesh):
    return jax.shard_map(
        on_device,
        mesh=mesh,
        in_specs=(P(AXES, None), P(AXES, None), P(), P()),
        out_specs=(P(AXES, None), P(AXES, None)),
        check_vma=False,
    )
```

```python
import functools

import jax
import jax.numpy as jnp
from jax import lax
from jax.experimental import pallas as pl
from jax.experimental.pallas import tpu as pltpu
from jax.sharding import PartitionSpec as P

AXES = ("blk", "group")
EPSILON = 1e-06
CHIPS = 4

SMEM = pl.BlockSpec(memory_space=pltpu.SMEM)
WHOLE = pl.BlockSpec(memory_space=pltpu.VMEM)


def params(mib):
    return pltpu.CompilerParams(vmem_limit_bytes=mib * 1024 * 1024)


def near_to(b, g, size):
    to = (b + 2) % size
    return to, g ^ (to // (2 * CHIPS) != b // (2 * CHIPS))


def guest_to(b, g, size):
    if b % 2 == 1:
        return None
    return (b - 1 if b // 2 % CHIPS > 0 else b + 2), g


def guest_partner_to(b, g, size):
    return (guest_to(b, g, size)[0], g ^ 1) if b % 2 == 0 else None


def far_to(b, g, size):
    return ((b + 5) % size, g ^ 1) if b % 2 == 1 and b // 2 % CHIPS == CHIPS - 2 else None


def other_core(b, g, size):
    return b ^ 1, g


def partner(b, g, size):
    return b, g ^ 1


def move(values, where, inverse=False):
    n_blk, n_group = lax.axis_size("blk"), lax.axis_size("group")
    pairs = []
    for b in range(n_blk):
        for g in range(n_group):
            to = where(b, g, n_blk)
            if to is not None:
                pair = (b * n_group + g, to[0] * n_group + to[1])
                pairs.append(pair[::-1] if inverse else pair)
    return lax.ppermute(values, AXES, sorted(pairs))


def normalize(values):
    full = values.astype(jnp.float32)
    inverse = lax.rsqrt(jnp.sum(full * full, axis=-1, keepdims=True) + EPSILON)
    return full * inverse, inverse


def hat(values):
    return normalize(values)[0].astype(jnp.bfloat16)


def dot(left, right, left_dim, right_dim):
    return lax.dot_general(
        left, right, (((left_dim,), (right_dim,)), ((), ())), preferred_element_type=jnp.float32
    )


def slopes_of(text_hat, image_hat, scale, bias, same=None):
    half = 0.5 * scale
    slopes = half * jnp.tanh(half * dot(text_hat, image_hat, 1, 1) + 0.5 * bias) + half
    if same is not None:
        slopes = slopes - scale * same
    return slopes.astype(jnp.bfloat16)


def rows_of(ref):
    count, rows, width = ref.shape
    return ref[...].reshape(count * rows, width)


def is_odd(role):
    return role[0] == 1


def has_guests(role):
    return jnp.logical_and(role[0] == 1, role[1] < CHIPS - 1)


def takes_far(role):
    return jnp.logical_and(role[0] == 0, role[1] == 1)


def pass_on(role, role_out):
    role_out[0] = role[0]
    role_out[1] = role[1]


def hats_kernel(image_ref, partner_ref, hats_ref):
    hats_ref[0] = hat(image_ref[...])
    hats_ref[1] = hat(partner_ref[...])


def near_kernel(
    role, scale_ref, bias_ref, text_ref, mine_ref, theirs_ref, guest_ref, guest_partner_ref, far_ref,
    role_out, grad_ref, hat_ref, mine_slopes_ref, theirs_slopes_ref, back_ref, back_partner_ref, far_grad_ref,
    total, guests_ref,
):
    pass_on(role, role_out)
    scale, bias = scale_ref[0], bias_ref[0]
    rows, width = hat_ref.shape
    near_hat = hat(text_ref[...])
    hat_ref[...] = near_hat
    mine, theirs = rows_of(mine_ref), rows_of(theirs_ref)
    mine_slopes = slopes_of(near_hat, mine, scale, bias)
    mine_slopes_ref[...] = mine_slopes
    theirs_slopes = slopes_of(near_hat, theirs, scale, bias)
    theirs_slopes_ref[...] = theirs_slopes
    total[...] = dot(mine_slopes, mine, 1, 0) + dot(theirs_slopes, theirs, 1, 0)

    def visits(text_hat):
        guests_ref[0] = hat(guest_ref[...])
        guests_ref[1] = hat(guest_partner_ref[...])
        guests = rows_of(guests_ref)
        slopes = slopes_of(text_hat, guests, scale, bias)
        back_ref[...] = dot(slopes[:, :rows], text_hat, 0, 0).astype(back_ref.dtype)
        back_partner_ref[...] = dot(slopes[:, rows:], text_hat, 0, 0).astype(back_partner_ref.dtype)
        return slopes, guests

    @pl.when(has_guests(role))
    def _():
        slopes, guests = visits(hat_ref[...])
        total[...] += dot(slopes, guests, 1, 0)

    @pl.when(takes_far(role))
    def _():
        slopes, guests = visits(hat(far_ref[...]))
        far_grad_ref[...] = dot(slopes, guests, 1, 0).astype(far_grad_ref.dtype)

    grad_ref[...] = total[...].astype(grad_ref.dtype)


def own_kernel(
    role, scale_ref, bias_ref, text_ref, mine_ref, theirs_ref, hat_ref,
    mine_slopes_ref, theirs_slopes_ref,
    text_sum_ref, mine_sum_ref, partner_sum_ref, cross_ref,
):
    scale, bias = scale_ref[0], bias_ref[0]
    rows, width = text_ref.shape
    near_hat = hat_ref[...]
    text_hat = hat(text_ref[...])
    same = (
        lax.broadcasted_iota(jnp.int32, (rows, 2 * rows), 0)
        == lax.broadcasted_iota(jnp.int32, (rows, 2 * rows), 1)
    ).astype(jnp.float32)
    images = rows_of(mine_ref)
    slopes = slopes_of(text_hat, images, scale, bias, same)
    text_sum_ref[...] = dot(slopes, images, 1, 0)
    for slot, out_ref in enumerate((mine_sum_ref, partner_sum_ref)):
        at = slice(slot * rows, (slot + 1) * rows)
        out_ref[...] = dot(slopes[:, at], text_hat, 0, 0) + dot(mine_slopes_ref[:, at], near_hat, 0, 0)

    @pl.when(role[0] == 0)
    def _():
        text_hat = hat(text_ref[...])
        images = rows_of(theirs_ref)
        own = slopes_of(text_hat, images, scale, bias)
        text_sum_ref[...] += dot(own, images, 1, 0)
        for slot in range(2):
            at = slice(slot * rows, (slot + 1) * rows)
            total = dot(theirs_slopes_ref[:, at], hat_ref[...], 0, 0) + dot(own[:, at], text_hat, 0, 0)
            cross_ref[slot] = total.astype(cross_ref.dtype)

    @pl.when(role[0] == 1)
    def _():
        for slot in range(2):
            at = slice(slot * rows, (slot + 1) * rows)
            cross_ref[slot] = dot(theirs_slopes_ref[:, at], hat_ref[...], 0, 0).astype(cross_ref.dtype)


def partner_kernel(role, sum_ref, cross_ref, back_ref, out_ref):
    even = 1.0 - is_odd(role).astype(jnp.float32)
    total = sum_ref[...] + cross_ref[0].astype(jnp.float32) + even * back_ref[...].astype(jnp.float32)
    out_ref[...] = total.astype(out_ref.dtype)


def project(raw, total):
    unit, inverse = normalize(raw)
    return (total - unit * jnp.sum(unit * total, axis=-1, keepdims=True)) * inverse


def text_final_kernel(role, texts, text_sum, near_back, far_back, role_out, out_ref):
    pass_on(role, role_out)
    total = text_sum[...] + near_back[...].astype(jnp.float32) + far_back[...].astype(jnp.float32)
    out_ref[...] = project(texts[...], total)


def image_final_kernel(role, images, image_sum, from_partner, out_ref):
    total = image_sum[...] + from_partner[...].astype(jnp.float32)
    out_ref[...] = project(images[...], total)


def call(kernel, out_shape, *operands, mib=16, scalars=3, scalar_outs=0, scratch=()):
    outs = out_shape if isinstance(out_shape, list) else [out_shape]
    out_specs = [SMEM] * scalar_outs + [WHOLE] * (len(outs) - scalar_outs)
    return pl.pallas_call(
        kernel,
        in_specs=[SMEM] * scalars + [WHOLE] * (len(operands) - scalars),
        out_specs=out_specs if isinstance(out_shape, list) else out_specs[0],
        out_shape=out_shape,
        scratch_shapes=list(scratch),
        compiler_params=params(mib),
    )(*operands)


def on_device(images, texts, logit_scale, logit_bias):
    rows, width = images.shape
    bf16 = functools.partial(jax.ShapeDtypeStruct, dtype=jnp.bfloat16)
    full = jax.ShapeDtypeStruct((rows, width), jnp.float32)
    half = bf16((rows, width))
    half_pair = bf16((2, rows, width))

    index = lax.axis_index("blk")
    role = jnp.stack([index % 2, index // 2 % CHIPS]).astype(jnp.int32)
    scalars = (role, logit_scale, logit_bias)
    positive = logit_scale[0] > 0

    def together(body, *operands):
        return lax.cond(positive, body, body, *operands)

    partner_images = move(images, partner)
    near = move(texts, near_to)
    guest = move(images, guest_to)
    guest_partner = move(images, guest_partner_to)
    far = move(texts, far_to)
    mine = call(hats_kernel, half_pair, images, partner_images, scalars=0)
    theirs = together(lambda values: move(values, other_core), mine)
    role_type = jax.ShapeDtypeStruct((2,), jnp.int32)
    scalars = (role, logit_scale, logit_bias)
    slopes_pair = bf16((rows, 2 * rows))
    role, near_grad, near_hat, mine_slopes, theirs_slopes, back, back_partner, far_grad = call(
        near_kernel,
        [role_type, half, half, slopes_pair, slopes_pair, half, half, half],
        *scalars, near, mine, theirs, guest, guest_partner, far,
        scratch=[pltpu.VMEM((rows, width), jnp.float32), pltpu.VMEM((2, rows, width), jnp.bfloat16)],
        mib=24,
        scalar_outs=1,
    )
    scalars = (role, logit_scale, logit_bias)
    near_back = move(near_grad, near_to, True)
    far_back = move(far_grad, far_to, True)
    back_partner = move(back_partner, guest_to, True)
    back = move(back, guest_to, True)
    text_sum, mine_sum, partner_sum, cross = call(
        own_kernel,
        [full, full, full, half_pair],
        *scalars, texts, mine, theirs, near_hat, mine_slopes, theirs_slopes,
        mib=24,
    )

    def sum_with_cross(kernel, slot, dtype, *operands):
        specs = []
        for operand in operands:
            if operand.shape == (2,):
                specs.append(SMEM)
            elif operand.ndim == 3:
                specs.append(pl.BlockSpec((1, rows, width), lambda i: (slot, 0, 0)))
            else:
                specs.append(pl.BlockSpec(operand.shape, lambda i: (0, 0)))
        return pl.pallas_call(
            kernel,
            grid=(1,),
            in_specs=specs,
            out_specs=pl.BlockSpec((rows, width), lambda i: (0, 0)),
            out_shape=jax.ShapeDtypeStruct((rows, width), dtype),
            compiler_params=params(16),
        )(*operands)

    def across(cross, role, partner_sum, back_partner):
        cross = move(cross, other_core)
        return cross, sum_with_cross(partner_kernel, 1, jnp.bfloat16, role, partner_sum, cross, back_partner)

    cross, for_partner = together(across, cross, role, partner_sum, back_partner)
    from_partner = move(for_partner, partner)
    image_sum = sum_with_cross(partner_kernel, 0, jnp.float32, role, mine_sum, cross, back)
    role, text_grad = call(
        text_final_kernel,
        [jax.ShapeDtypeStruct((2,), jnp.int32), full],
        role, texts, text_sum, near_back, far_back,
        scalars=1, scalar_outs=1,
    )
    image_grad = call(image_final_kernel, full, role, images, image_sum, from_partner, scalars=1)
    return image_grad, text_grad


def solution(mesh):
    return jax.shard_map(
        on_device,
        mesh=mesh,
        in_specs=(P(AXES, None), P(AXES, None), P(), P()),
        out_specs=(P(AXES, None), P(AXES, None)),
        check_vma=False,
    )
```

```python
import functools

import jax
import jax.numpy as jnp
from jax import lax
from jax.experimental import pallas as pl
from jax.experimental.pallas import tpu as pltpu
from jax.sharding import PartitionSpec as P

AXES = ("blk", "group")
EPSILON = 1e-06
CHIPS = 4

SMEM = pl.BlockSpec(memory_space=pltpu.SMEM)
WHOLE = pl.BlockSpec(memory_space=pltpu.VMEM)


def params(mib):
    return pltpu.CompilerParams(vmem_limit_bytes=mib * 1024 * 1024)


def near_to(b, g, size):
    to = (b + 2) % size
    return to, g ^ (to // (2 * CHIPS) != b // (2 * CHIPS))


def guest_to(b, g, size):
    if b % 2 == 1:
        return None
    return (b - 1 if b // 2 % CHIPS > 0 else b + 2), g


def guest_partner_to(b, g, size):
    return (guest_to(b, g, size)[0], g ^ 1) if b % 2 == 0 else None


def far_to(b, g, size):
    return ((b + 5) % size, g ^ 1) if b % 2 == 1 and b // 2 % CHIPS == CHIPS - 2 else None


def back_to(b, g, size):
    to = (b - 2) % size
    if to // (2 * CHIPS) == b // (2 * CHIPS):
        return to, g
    return (to, g ^ 1) if b % 2 == 0 else (b + 2 * CHIPS - 2, g)


def over_z(b, g, size):
    return ((b + 2 * CHIPS) % size, g ^ 1) if b % 2 == 1 and b // 2 % CHIPS == CHIPS - 1 else None


def other_core(b, g, size):
    return b ^ 1, g


def partner(b, g, size):
    return b, g ^ 1


def move(values, where, inverse=False):
    n_blk, n_group = lax.axis_size("blk"), lax.axis_size("group")
    pairs = []
    for b in range(n_blk):
        for g in range(n_group):
            to = where(b, g, n_blk)
            if to is not None:
                pair = (b * n_group + g, to[0] * n_group + to[1])
                pairs.append(pair[::-1] if inverse else pair)
    return lax.ppermute(values, AXES, sorted(pairs))


def normalize(values):
    full = values.astype(jnp.float32)
    inverse = lax.rsqrt(jnp.sum(full * full, axis=-1, keepdims=True) + EPSILON)
    return full * inverse, inverse


def hat(values):
    return normalize(values)[0].astype(jnp.bfloat16)


def dot(left, right, left_dim, right_dim):
    return lax.dot_general(
        left, right, (((left_dim,), (right_dim,)), ((), ())), preferred_element_type=jnp.float32
    )


def slopes_of(text_hat, image_hat, scale, bias, same=None):
    half = 0.5 * scale
    slopes = half * jnp.tanh(half * dot(text_hat, image_hat, 1, 1) + 0.5 * bias) + half
    if same is not None:
        slopes = slopes - scale * same
    return slopes.astype(jnp.bfloat16)


def rows_of(ref):
    count, rows, width = ref.shape
    return ref[...].reshape(count * rows, width)


def is_odd(role):
    return role[0] == 1


def has_guests(role):
    return jnp.logical_and(role[0] == 1, role[1] < CHIPS - 1)


def takes_far(role):
    return jnp.logical_and(role[0] == 0, role[1] == 1)


def pass_on(role, role_out):
    role_out[0] = role[0]
    role_out[1] = role[1]


def hats_kernel(image_ref, partner_ref, hats_ref):
    hats_ref[0] = hat(image_ref[...])
    hats_ref[1] = hat(partner_ref[...])


def near_kernel(
    role, scale_ref, bias_ref, text_ref, mine_ref, theirs_ref, guest_ref, guest_partner_ref, far_ref,
    role_out, grad_ref, hat_ref, mine_slopes_ref, theirs_slopes_ref, back_ref, back_partner_ref, far_grad_ref,
    total, guests_ref,
):
    pass_on(role, role_out)
    scale, bias = scale_ref[0], bias_ref[0]
    rows, width = hat_ref.shape
    near_hat = hat(text_ref[...])
    hat_ref[...] = near_hat
    mine, theirs = rows_of(mine_ref), rows_of(theirs_ref)
    mine_slopes = slopes_of(near_hat, mine, scale, bias)
    mine_slopes_ref[...] = mine_slopes
    theirs_slopes = slopes_of(near_hat, theirs, scale, bias)
    theirs_slopes_ref[...] = theirs_slopes
    total[...] = dot(mine_slopes, mine, 1, 0) + dot(theirs_slopes, theirs, 1, 0)

    def visits(text_hat):
        guests_ref[0] = hat(guest_ref[...])
        guests_ref[1] = hat(guest_partner_ref[...])
        guests = rows_of(guests_ref)
        slopes = slopes_of(text_hat, guests, scale, bias)
        back_ref[...] = dot(slopes[:, :rows], text_hat, 0, 0).astype(back_ref.dtype)
        back_partner_ref[...] = dot(slopes[:, rows:], text_hat, 0, 0).astype(back_partner_ref.dtype)
        return slopes, guests

    @pl.when(has_guests(role))
    def _():
        slopes, guests = visits(hat_ref[...])
        total[...] += dot(slopes, guests, 1, 0)

    @pl.when(takes_far(role))
    def _():
        slopes, guests = visits(hat(far_ref[...]))
        far_grad_ref[...] = dot(slopes, guests, 1, 0).astype(far_grad_ref.dtype)

    grad_ref[...] = total[...].astype(grad_ref.dtype)


def own_kernel(
    role, scale_ref, bias_ref, text_ref, mine_ref, theirs_ref, hat_ref,
    mine_slopes_ref, theirs_slopes_ref,
    text_sum_ref, mine_sum_ref, partner_sum_ref, cross_ref,
):
    scale, bias = scale_ref[0], bias_ref[0]
    rows, width = text_ref.shape
    near_hat = hat_ref[...]
    text_hat = hat(text_ref[...])
    same = (
        lax.broadcasted_iota(jnp.int32, (rows, 2 * rows), 0)
        == lax.broadcasted_iota(jnp.int32, (rows, 2 * rows), 1)
    ).astype(jnp.float32)
    images = rows_of(mine_ref)
    slopes = slopes_of(text_hat, images, scale, bias, same)
    text_sum_ref[...] = dot(slopes, images, 1, 0)
    for slot, out_ref in enumerate((mine_sum_ref, partner_sum_ref)):
        at = slice(slot * rows, (slot + 1) * rows)
        out_ref[...] = dot(slopes[:, at], text_hat, 0, 0) + dot(mine_slopes_ref[:, at], near_hat, 0, 0)

    @pl.when(role[0] == 0)
    def _():
        text_hat = hat(text_ref[...])
        images = rows_of(theirs_ref)
        own = slopes_of(text_hat, images, scale, bias)
        text_sum_ref[...] += dot(own, images, 1, 0)
        for slot in range(2):
            at = slice(slot * rows, (slot + 1) * rows)
            total = dot(theirs_slopes_ref[:, at], hat_ref[...], 0, 0) + dot(own[:, at], text_hat, 0, 0)
            cross_ref[slot] = total.astype(cross_ref.dtype)

    @pl.when(role[0] == 1)
    def _():
        for slot in range(2):
            at = slice(slot * rows, (slot + 1) * rows)
            cross_ref[slot] = dot(theirs_slopes_ref[:, at], hat_ref[...], 0, 0).astype(cross_ref.dtype)


def partner_kernel(role, sum_ref, cross_ref, back_ref, out_ref):
    even = 1.0 - is_odd(role).astype(jnp.float32)
    total = sum_ref[...] + cross_ref[0].astype(jnp.float32) + even * back_ref[...].astype(jnp.float32)
    out_ref[...] = total.astype(out_ref.dtype)


def project(raw, total):
    unit, inverse = normalize(raw)
    return (total - unit * jnp.sum(unit * total, axis=-1, keepdims=True)) * inverse


def text_final_kernel(role, texts, text_sum, near_back, last_back, far_back, role_out, out_ref):
    pass_on(role, role_out)
    last = jnp.logical_and(role[0] == 1, role[1] == CHIPS - 1)
    near = jnp.where(last, last_back[...].astype(jnp.float32), near_back[...].astype(jnp.float32))
    total = text_sum[...] + near + far_back[...].astype(jnp.float32)
    out_ref[...] = project(texts[...], total)


def image_final_kernel(role, images, image_sum, from_partner, out_ref):
    total = image_sum[...] + from_partner[...].astype(jnp.float32)
    out_ref[...] = project(images[...], total)


def call(kernel, out_shape, *operands, mib=16, scalars=3, scalar_outs=0, scratch=()):
    outs = out_shape if isinstance(out_shape, list) else [out_shape]
    out_specs = [SMEM] * scalar_outs + [WHOLE] * (len(outs) - scalar_outs)
    return pl.pallas_call(
        kernel,
        in_specs=[SMEM] * scalars + [WHOLE] * (len(operands) - scalars),
        out_specs=out_specs if isinstance(out_shape, list) else out_specs[0],
        out_shape=out_shape,
        scratch_shapes=list(scratch),
        compiler_params=params(mib),
    )(*operands)


def on_device(images, texts, logit_scale, logit_bias):
    rows, width = images.shape
    bf16 = functools.partial(jax.ShapeDtypeStruct, dtype=jnp.bfloat16)
    full = jax.ShapeDtypeStruct((rows, width), jnp.float32)
    half = bf16((rows, width))
    half_pair = bf16((2, rows, width))

    index = lax.axis_index("blk")
    role = jnp.stack([index % 2, index // 2 % CHIPS]).astype(jnp.int32)
    scalars = (role, logit_scale, logit_bias)
    positive = logit_scale[0] > 0

    def together(body, *operands):
        return lax.cond(positive, body, body, *operands)

    partner_images = move(images, partner)
    near = move(texts, near_to)
    guest = move(images, guest_to)
    guest_partner = move(images, guest_partner_to)
    far = move(texts, far_to)
    mine = call(hats_kernel, half_pair, images, partner_images, scalars=0)
    theirs = together(lambda values: move(values, other_core), mine)
    role_type = jax.ShapeDtypeStruct((2,), jnp.int32)
    scalars = (role, logit_scale, logit_bias)
    slopes_pair = bf16((rows, 2 * rows))
    role, near_grad, near_hat, mine_slopes, theirs_slopes, back, back_partner, far_grad = call(
        near_kernel,
        [role_type, half, half, slopes_pair, slopes_pair, half, half, half],
        *scalars, near, mine, theirs, guest, guest_partner, far,
        scratch=[pltpu.VMEM((rows, width), jnp.float32), pltpu.VMEM((2, rows, width), jnp.bfloat16)],
        mib=24,
        scalar_outs=1,
    )
    scalars = (role, logit_scale, logit_bias)
    near_back = move(near_grad, back_to)
    far_back = move(far_grad, far_to, True)
    back_partner = move(back_partner, guest_to, True)
    back = move(back, guest_to, True)
    text_sum, mine_sum, partner_sum, cross = call(
        own_kernel,
        [full, full, full, half_pair],
        *scalars, texts, mine, theirs, near_hat, mine_slopes, theirs_slopes,
        mib=24,
    )

    def sum_with_cross(kernel, slot, dtype, *operands):
        specs = []
        for operand in operands:
            if operand.shape == (2,):
                specs.append(SMEM)
            elif operand.ndim == 3:
                specs.append(pl.BlockSpec((1, rows, width), lambda i: (slot, 0, 0)))
            else:
                specs.append(pl.BlockSpec(operand.shape, lambda i: (0, 0)))
        return pl.pallas_call(
            kernel,
            grid=(1,),
            in_specs=specs,
            out_specs=pl.BlockSpec((rows, width), lambda i: (0, 0)),
            out_shape=jax.ShapeDtypeStruct((rows, width), dtype),
            compiler_params=params(16),
        )(*operands)

    def across(cross, role, partner_sum, back_partner):
        cross = move(cross, other_core)
        return cross, sum_with_cross(partner_kernel, 1, jnp.bfloat16, role, partner_sum, cross, back_partner)

    cross, for_partner = together(across, cross, role, partner_sum, back_partner)
    from_partner = move(for_partner, partner)
    last_back = together(lambda values: move(values, over_z), near_back)
    image_sum = sum_with_cross(partner_kernel, 0, jnp.float32, role, mine_sum, cross, back)
    role, text_grad = call(
        text_final_kernel,
        [jax.ShapeDtypeStruct((2,), jnp.int32), full],
        role, texts, text_sum, near_back, last_back, far_back,
        scalars=1, scalar_outs=1,
    )
    image_grad = call(image_final_kernel, full, role, images, image_sum, from_partner, scalars=1)
    return image_grad, text_grad


def solution(mesh):
    return jax.shard_map(
        on_device,
        mesh=mesh,
        in_specs=(P(AXES, None), P(AXES, None), P(), P()),
        out_specs=(P(AXES, None), P(AXES, None)),
        check_vma=False,
    )
```

```python
import functools

import jax
import jax.numpy as jnp
from jax import lax
from jax.experimental import pallas as pl
from jax.experimental.pallas import tpu as pltpu
from jax.sharding import PartitionSpec as P

AXES = ("blk", "group")
EPSILON = 1e-06
CHIPS = 4

SMEM = pl.BlockSpec(memory_space=pltpu.SMEM)
WHOLE = pl.BlockSpec(memory_space=pltpu.VMEM)


def params(mib):
    return pltpu.CompilerParams(vmem_limit_bytes=mib * 1024 * 1024)


def near_to(b, g, size):
    to = (b + 2) % size
    return to, g ^ (to // (2 * CHIPS) != b // (2 * CHIPS))


def guest_to(b, g, size):
    if b % 2 == 1:
        return None
    return (b - 1 if b // 2 % CHIPS > 0 else b + 2), g


def guest_partner_to(b, g, size):
    return (guest_to(b, g, size)[0], g ^ 1) if b % 2 == 0 else None


def far_to(b, g, size):
    return ((b + 5) % size, g ^ 1) if b % 2 == 1 and b // 2 % CHIPS == CHIPS - 2 else None


def back_to(b, g, size):
    to = (b - 2) % size
    if to // (2 * CHIPS) == b // (2 * CHIPS):
        return to, g
    return (to, g ^ 1) if b % 2 == 0 else (b + 2 * CHIPS - 2, g)


def over_z(b, g, size):
    return ((b + 2 * CHIPS) % size, g ^ 1) if b % 2 == 1 and b // 2 % CHIPS == CHIPS - 1 else None


def other_core(b, g, size):
    return b ^ 1, g


def partner(b, g, size):
    return b, g ^ 1


def move(values, where, inverse=False):
    n_blk, n_group = lax.axis_size("blk"), lax.axis_size("group")
    pairs = []
    for b in range(n_blk):
        for g in range(n_group):
            to = where(b, g, n_blk)
            if to is not None:
                pair = (b * n_group + g, to[0] * n_group + to[1])
                pairs.append(pair[::-1] if inverse else pair)
    return lax.ppermute(values, AXES, sorted(pairs))


def normalize(values):
    full = values.astype(jnp.float32)
    inverse = lax.rsqrt(jnp.sum(full * full, axis=-1, keepdims=True) + EPSILON)
    return full * inverse, inverse


def hat(values):
    return normalize(values)[0].astype(jnp.bfloat16)


def dot(left, right, left_dim, right_dim):
    return lax.dot_general(
        left, right, (((left_dim,), (right_dim,)), ((), ())), preferred_element_type=jnp.float32
    )


def slopes_of(text_hat, image_hat, scale, bias, same=None):
    half = 0.5 * scale
    slopes = half * jnp.tanh(half * dot(text_hat, image_hat, 1, 1) + 0.5 * bias) + half
    if same is not None:
        slopes = slopes - scale * same
    return slopes.astype(jnp.bfloat16)


def rows_of(ref):
    count, rows, width = ref.shape
    return ref[...].reshape(count * rows, width)


def is_odd(role):
    return role[0] == 1


def has_guests(role):
    return jnp.logical_and(role[0] == 1, role[1] < CHIPS - 1)


def takes_far(role):
    return jnp.logical_and(role[0] == 0, role[1] == 1)


def pass_on(role, role_out):
    role_out[0] = role[0]
    role_out[1] = role[1]


def hats_kernel(image_ref, partner_ref, hats_ref):
    hats_ref[0] = hat(image_ref[...])
    hats_ref[1] = hat(partner_ref[...])


def near_kernel(
    role, scale_ref, bias_ref, text_ref, mine_ref, theirs_ref, guest_ref, guest_partner_ref, far_ref,
    role_out, grad_ref, hat_ref, mine_slopes_ref, theirs_slopes_ref, back_ref, back_partner_ref, far_grad_ref,
    total, guests_ref,
):
    pass_on(role, role_out)
    scale, bias = scale_ref[0], bias_ref[0]
    rows, width = hat_ref.shape
    near_hat = hat(text_ref[...])
    hat_ref[...] = near_hat
    mine, theirs = rows_of(mine_ref), rows_of(theirs_ref)
    mine_slopes = slopes_of(near_hat, mine, scale, bias)
    mine_slopes_ref[...] = mine_slopes
    theirs_slopes = slopes_of(near_hat, theirs, scale, bias)
    theirs_slopes_ref[...] = theirs_slopes
    total[...] = dot(mine_slopes, mine, 1, 0) + dot(theirs_slopes, theirs, 1, 0)

    def visits(text_hat):
        guests_ref[0] = hat(guest_ref[...])
        guests_ref[1] = hat(guest_partner_ref[...])
        guests = rows_of(guests_ref)
        slopes = slopes_of(text_hat, guests, scale, bias)
        back_ref[...] = dot(slopes[:, :rows], text_hat, 0, 0).astype(back_ref.dtype)
        back_partner_ref[...] = dot(slopes[:, rows:], text_hat, 0, 0).astype(back_partner_ref.dtype)
        return slopes, guests

    @pl.when(has_guests(role))
    def _():
        slopes, guests = visits(hat_ref[...])
        total[...] += dot(slopes, guests, 1, 0)

    @pl.when(takes_far(role))
    def _():
        slopes, guests = visits(hat(far_ref[...]))
        far_grad_ref[...] = dot(slopes, guests, 1, 0).astype(far_grad_ref.dtype)

    grad_ref[...] = total[...].astype(grad_ref.dtype)


def sent_kernel(
    role, scale_ref, bias_ref, text_ref, mine_ref, theirs_ref, hat_ref, mine_slopes_ref, theirs_slopes_ref,
    cross_ref, partner_sum_ref, slopes_ref,
):
    scale, bias = scale_ref[0], bias_ref[0]
    rows, width = text_ref.shape
    text_hat = hat(text_ref[...])
    slopes = slopes_of(text_hat, mine_ref[1], scale, bias)
    slopes_ref[:, :rows] = slopes
    partner_sum_ref[...] = dot(slopes, text_hat, 0, 0) + dot(mine_slopes_ref[:, rows:], hat_ref[...], 0, 0)

    @pl.when(role[0] == 0)
    def _():
        text_hat = hat(text_ref[...])
        slopes = slopes_of(text_hat, rows_of(theirs_ref), scale, bias)
        slopes_ref[:, rows:] = slopes
        for slot in range(2):
            at = slice(slot * rows, (slot + 1) * rows)
            total = dot(theirs_slopes_ref[:, at], hat_ref[...], 0, 0) + dot(slopes[:, at], text_hat, 0, 0)
            cross_ref[slot] = total.astype(cross_ref.dtype)

    @pl.when(role[0] == 1)
    def _():
        for slot in range(2):
            at = slice(slot * rows, (slot + 1) * rows)
            cross_ref[slot] = dot(theirs_slopes_ref[:, at], hat_ref[...], 0, 0).astype(cross_ref.dtype)


def kept_kernel(
    role, scale_ref, bias_ref, text_ref, mine_ref, theirs_ref, hat_ref, slopes_ref, mine_slopes_ref, cross_ref, back_ref,
    text_sum_ref, image_sum_ref,
):
    scale, bias = scale_ref[0], bias_ref[0]
    rows, width = hat_ref.shape
    text_hat = hat(text_ref[...])
    same = (
        lax.broadcasted_iota(jnp.int32, (rows, rows), 0) == lax.broadcasted_iota(jnp.int32, (rows, rows), 1)
    ).astype(jnp.float32)
    slopes = slopes_of(text_hat, mine_ref[0], scale, bias, same)
    even = 1.0 - is_odd(role).astype(jnp.float32)
    image_sum_ref[...] = (
        dot(slopes, text_hat, 0, 0)
        + dot(mine_slopes_ref[:, :rows], hat_ref[...], 0, 0)
        + cross_ref[0].astype(jnp.float32)
        + even * back_ref[...].astype(jnp.float32)
    )
    text_sum_ref[...] = dot(slopes, mine_ref[0], 1, 0) + dot(slopes_ref[:, :rows], mine_ref[1], 1, 0)

    @pl.when(role[0] == 0)
    def _():
        text_sum_ref[...] += dot(slopes_ref[:, rows:], rows_of(theirs_ref), 1, 0)


def partner_kernel(role, sum_ref, cross_ref, back_ref, out_ref):
    even = 1.0 - is_odd(role).astype(jnp.float32)
    total = sum_ref[...] + cross_ref[0].astype(jnp.float32) + even * back_ref[...].astype(jnp.float32)
    out_ref[...] = total.astype(out_ref.dtype)


def project(raw, total):
    unit, inverse = normalize(raw)
    return (total - unit * jnp.sum(unit * total, axis=-1, keepdims=True)) * inverse


def text_final_kernel(role, texts, text_sum, near_back, last_back, far_back, role_out, out_ref):
    pass_on(role, role_out)
    last = jnp.logical_and(role[0] == 1, role[1] == CHIPS - 1)
    near = jnp.where(last, last_back[...].astype(jnp.float32), near_back[...].astype(jnp.float32))
    total = text_sum[...] + near + far_back[...].astype(jnp.float32)
    out_ref[...] = project(texts[...], total)


def image_final_kernel(role, images, image_sum, from_partner, out_ref):
    total = image_sum[...] + from_partner[...].astype(jnp.float32)
    out_ref[...] = project(images[...], total)


def call(kernel, out_shape, *operands, mib=16, scalars=3, scalar_outs=0, scratch=()):
    outs = out_shape if isinstance(out_shape, list) else [out_shape]
    out_specs = [SMEM] * scalar_outs + [WHOLE] * (len(outs) - scalar_outs)
    return pl.pallas_call(
        kernel,
        in_specs=[SMEM] * scalars + [WHOLE] * (len(operands) - scalars),
        out_specs=out_specs if isinstance(out_shape, list) else out_specs[0],
        out_shape=out_shape,
        scratch_shapes=list(scratch),
        compiler_params=params(mib),
    )(*operands)


def on_device(images, texts, logit_scale, logit_bias):
    rows, width = images.shape
    bf16 = functools.partial(jax.ShapeDtypeStruct, dtype=jnp.bfloat16)
    full = jax.ShapeDtypeStruct((rows, width), jnp.float32)
    half = bf16((rows, width))
    half_pair = bf16((2, rows, width))

    index = lax.axis_index("blk")
    role = jnp.stack([index % 2, index // 2 % CHIPS]).astype(jnp.int32)
    scalars = (role, logit_scale, logit_bias)
    positive = logit_scale[0] > 0

    def together(body, *operands):
        return lax.cond(positive, body, body, *operands)

    partner_images = move(images, partner)
    near = move(texts, near_to)
    guest = move(images, guest_to)
    guest_partner = move(images, guest_partner_to)
    far = move(texts, far_to)
    mine = call(hats_kernel, half_pair, images, partner_images, scalars=0)
    theirs = together(lambda values: move(values, other_core), mine)
    role_type = jax.ShapeDtypeStruct((2,), jnp.int32)
    scalars = (role, logit_scale, logit_bias)
    slopes_pair = bf16((rows, 2 * rows))
    role, near_grad, near_hat, mine_slopes, theirs_slopes, back, back_partner, far_grad = call(
        near_kernel,
        [role_type, half, half, slopes_pair, slopes_pair, half, half, half],
        *scalars, near, mine, theirs, guest, guest_partner, far,
        scratch=[pltpu.VMEM((rows, width), jnp.float32), pltpu.VMEM((2, rows, width), jnp.bfloat16)],
        mib=24,
        scalar_outs=1,
    )
    scalars = (role, logit_scale, logit_bias)
    near_back = move(near_grad, back_to)
    far_back = move(far_grad, far_to, True)
    back_partner = move(back_partner, guest_to, True)
    back = move(back, guest_to, True)
    cross, partner_sum, own_slopes = call(
        sent_kernel,
        [half_pair, full, bf16((rows, 3 * rows))],
        *scalars, texts, mine, theirs, near_hat, mine_slopes, theirs_slopes,
    )

    def sum_with_cross(kernel, slot, dtype, *operands):
        specs = []
        for operand in operands:
            if operand.shape == (2,):
                specs.append(SMEM)
            elif operand.ndim == 3:
                specs.append(pl.BlockSpec((1, rows, width), lambda i: (slot, 0, 0)))
            else:
                specs.append(pl.BlockSpec(operand.shape, lambda i: (0, 0)))
        return pl.pallas_call(
            kernel,
            grid=(1,),
            in_specs=specs,
            out_specs=pl.BlockSpec((rows, width), lambda i: (0, 0)),
            out_shape=jax.ShapeDtypeStruct((rows, width), dtype),
            compiler_params=params(16),
        )(*operands)

    def across(cross, role, partner_sum, back_partner):
        cross = move(cross, other_core)
        return cross, sum_with_cross(partner_kernel, 1, jnp.bfloat16, role, partner_sum, cross, back_partner)

    cross, for_partner = together(across, cross, role, partner_sum, back_partner)
    from_partner = move(for_partner, partner)
    def over(near_back, *kept):
        text_sum, image_sum = call(kept_kernel, [full, full], *kept, mib=20)
        return move(near_back, over_z), text_sum, image_sum

    last_back, text_sum, image_sum = together(
        over, near_back, *scalars, texts, mine, theirs, near_hat, own_slopes, mine_slopes, cross, back
    )
    role, text_grad = call(
        text_final_kernel,
        [jax.ShapeDtypeStruct((2,), jnp.int32), full],
        role, texts, text_sum, near_back, last_back, far_back,
        scalars=1, scalar_outs=1,
    )
    image_grad = call(image_final_kernel, full, role, images, image_sum, from_partner, scalars=1)
    return image_grad, text_grad


def solution(mesh):
    return jax.shard_map(
        on_device,
        mesh=mesh,
        in_specs=(P(AXES, None), P(AXES, None), P(), P()),
        out_specs=(P(AXES, None), P(AXES, None)),
        check_vma=False,
    )
```

```python
import functools

import jax
import jax.numpy as jnp
from jax import lax
from jax.experimental import pallas as pl
from jax.experimental.pallas import tpu as pltpu
from jax.sharding import PartitionSpec as P

AXES = ("blk", "group")
EPSILON = 1e-06
CHIPS = 4

SMEM = pl.BlockSpec(memory_space=pltpu.SMEM)
WHOLE = pl.BlockSpec(memory_space=pltpu.VMEM)


def params(mib):
    return pltpu.CompilerParams(vmem_limit_bytes=mib * 1024 * 1024)


def near_to(b, g, size):
    to = (b + 2) % size
    return to, g ^ (to // (2 * CHIPS) != b // (2 * CHIPS))


def guest_to(b, g, size):
    if b % 2 == 1:
        return None
    return (b - 1 if b // 2 % CHIPS > 0 else b + 2), g


def guest_partner_to(b, g, size):
    return (guest_to(b, g, size)[0], g ^ 1) if b % 2 == 0 else None


def far_to(b, g, size):
    return ((b + 5) % size, g ^ 1) if b % 2 == 1 and b // 2 % CHIPS == CHIPS - 2 else None


def back_to(b, g, size):
    to = (b - 2) % size
    if to // (2 * CHIPS) == b // (2 * CHIPS):
        return to, g
    return (to, g ^ 1) if b % 2 == 0 else (b + 2 * CHIPS - 2, g)


def over_z(b, g, size):
    return ((b + 2 * CHIPS) % size, g ^ 1) if b % 2 == 1 and b // 2 % CHIPS == CHIPS - 1 else None


def other_core(b, g, size):
    return b ^ 1, g


def partner(b, g, size):
    return b, g ^ 1


def move(values, where, inverse=False):
    n_blk, n_group = lax.axis_size("blk"), lax.axis_size("group")
    pairs = []
    for b in range(n_blk):
        for g in range(n_group):
            to = where(b, g, n_blk)
            if to is not None:
                pair = (b * n_group + g, to[0] * n_group + to[1])
                pairs.append(pair[::-1] if inverse else pair)
    return lax.ppermute(values, AXES, sorted(pairs))


def normalize(values):
    full = values.astype(jnp.float32)
    inverse = lax.rsqrt(jnp.sum(full * full, axis=-1, keepdims=True) + EPSILON)
    return full * inverse, inverse


def hat(values):
    return normalize(values)[0].astype(jnp.bfloat16)


def dot(left, right, left_dim, right_dim):
    return lax.dot_general(
        left, right, (((left_dim,), (right_dim,)), ((), ())), preferred_element_type=jnp.float32
    )


def slopes_of(text_hat, image_hat, scale, bias, same=None):
    half = 0.5 * scale
    slopes = half * jnp.tanh(half * dot(text_hat, image_hat, 1, 1) + 0.5 * bias) + half
    if same is not None:
        slopes = slopes - scale * same
    return slopes.astype(jnp.bfloat16)


def rows_of(ref):
    count, rows, width = ref.shape
    return ref[...].reshape(count * rows, width)


def is_odd(role):
    return role[0] == 1


def has_guests(role):
    return jnp.logical_and(role[0] == 1, role[1] < CHIPS - 1)


def takes_far(role):
    return jnp.logical_and(role[0] == 0, role[1] == 1)


def pass_on(role, role_out):
    role_out[0] = role[0]
    role_out[1] = role[1]


def near_hat_kernel(role, text_ref, role_out, hat_ref):
    pass_on(role, role_out)
    hat_ref[...] = hat(text_ref[...])


def hats_kernel(image_ref, partner_ref, hats_ref):
    hats_ref[0] = hat(image_ref[...])
    hats_ref[1] = hat(partner_ref[...])


def near_kernel(
    role, scale_ref, bias_ref, hat_ref, mine_ref, theirs_ref, guest_ref, guest_partner_ref, far_ref,
    role_out, grad_ref, mine_slopes_ref, theirs_slopes_ref, back_ref, back_partner_ref, far_grad_ref,
    total, guests_ref,
):
    pass_on(role, role_out)
    scale, bias = scale_ref[0], bias_ref[0]
    rows, width = hat_ref.shape
    near_hat = hat_ref[...]
    mine, theirs = rows_of(mine_ref), rows_of(theirs_ref)
    mine_slopes = slopes_of(near_hat, mine, scale, bias)
    mine_slopes_ref[...] = mine_slopes
    theirs_slopes = slopes_of(near_hat, theirs, scale, bias)
    theirs_slopes_ref[...] = theirs_slopes
    total[...] = dot(mine_slopes, mine, 1, 0) + dot(theirs_slopes, theirs, 1, 0)

    def visits(text_hat):
        guests_ref[0] = hat(guest_ref[...])
        guests_ref[1] = hat(guest_partner_ref[...])
        guests = rows_of(guests_ref)
        slopes = slopes_of(text_hat, guests, scale, bias)
        back_ref[...] = dot(slopes[:, :rows], text_hat, 0, 0).astype(back_ref.dtype)
        back_partner_ref[...] = dot(slopes[:, rows:], text_hat, 0, 0).astype(back_partner_ref.dtype)
        return slopes, guests

    @pl.when(has_guests(role))
    def _():
        slopes, guests = visits(hat_ref[...])
        total[...] += dot(slopes, guests, 1, 0)

    @pl.when(takes_far(role))
    def _():
        slopes, guests = visits(hat(far_ref[...]))
        far_grad_ref[...] = dot(slopes, guests, 1, 0).astype(far_grad_ref.dtype)

    grad_ref[...] = total[...].astype(grad_ref.dtype)


def sent_kernel(
    role, scale_ref, bias_ref, text_ref, mine_ref, theirs_ref, hat_ref, mine_slopes_ref, theirs_slopes_ref,
    cross_ref, partner_sum_ref, slopes_ref,
):
    scale, bias = scale_ref[0], bias_ref[0]
    rows, width = text_ref.shape
    text_hat = hat(text_ref[...])
    slopes = slopes_of(text_hat, mine_ref[1], scale, bias)
    slopes_ref[:, :rows] = slopes
    partner_sum_ref[...] = dot(slopes, text_hat, 0, 0) + dot(mine_slopes_ref[:, rows:], hat_ref[...], 0, 0)

    @pl.when(role[0] == 0)
    def _():
        text_hat = hat(text_ref[...])
        slopes = slopes_of(text_hat, rows_of(theirs_ref), scale, bias)
        slopes_ref[:, rows:] = slopes
        for slot in range(2):
            at = slice(slot * rows, (slot + 1) * rows)
            total = dot(theirs_slopes_ref[:, at], hat_ref[...], 0, 0) + dot(slopes[:, at], text_hat, 0, 0)
            cross_ref[slot] = total.astype(cross_ref.dtype)

    @pl.when(role[0] == 1)
    def _():
        for slot in range(2):
            at = slice(slot * rows, (slot + 1) * rows)
            cross_ref[slot] = dot(theirs_slopes_ref[:, at], hat_ref[...], 0, 0).astype(cross_ref.dtype)


def kept_kernel(
    role, scale_ref, bias_ref, text_ref, mine_ref, theirs_ref, hat_ref, slopes_ref, mine_slopes_ref, cross_ref, back_ref,
    text_sum_ref, image_sum_ref,
):
    scale, bias = scale_ref[0], bias_ref[0]
    rows, width = hat_ref.shape
    text_hat = hat(text_ref[...])
    same = (
        lax.broadcasted_iota(jnp.int32, (rows, rows), 0) == lax.broadcasted_iota(jnp.int32, (rows, rows), 1)
    ).astype(jnp.float32)
    slopes = slopes_of(text_hat, mine_ref[0], scale, bias, same)
    even = 1.0 - is_odd(role).astype(jnp.float32)
    image_sum_ref[...] = (
        dot(slopes, text_hat, 0, 0)
        + dot(mine_slopes_ref[:, :rows], hat_ref[...], 0, 0)
        + cross_ref[0].astype(jnp.float32)
        + even * back_ref[...].astype(jnp.float32)
    )
    text_sum_ref[...] = dot(slopes, mine_ref[0], 1, 0) + dot(slopes_ref[:, :rows], mine_ref[1], 1, 0)

    @pl.when(role[0] == 0)
    def _():
        text_sum_ref[...] += dot(slopes_ref[:, rows:], rows_of(theirs_ref), 1, 0)


def partner_kernel(role, sum_ref, cross_ref, back_ref, out_ref):
    even = 1.0 - is_odd(role).astype(jnp.float32)
    total = sum_ref[...] + cross_ref[0].astype(jnp.float32) + even * back_ref[...].astype(jnp.float32)
    out_ref[...] = total.astype(out_ref.dtype)


def project(raw, total):
    unit, inverse = normalize(raw)
    return (total - unit * jnp.sum(unit * total, axis=-1, keepdims=True)) * inverse


def text_final_kernel(role, texts, text_sum, near_back, last_back, far_back, role_out, out_ref):
    pass_on(role, role_out)
    last = jnp.logical_and(role[0] == 1, role[1] == CHIPS - 1)
    near = jnp.where(last, last_back[...].astype(jnp.float32), near_back[...].astype(jnp.float32))
    total = text_sum[...] + near + far_back[...].astype(jnp.float32)
    out_ref[...] = project(texts[...], total)


def image_final_kernel(role, images, image_sum, from_partner, out_ref):
    total = image_sum[...] + from_partner[...].astype(jnp.float32)
    out_ref[...] = project(images[...], total)


def call(kernel, out_shape, *operands, mib=16, scalars=3, scalar_outs=0, scratch=()):
    outs = out_shape if isinstance(out_shape, list) else [out_shape]
    out_specs = [SMEM] * scalar_outs + [WHOLE] * (len(outs) - scalar_outs)
    return pl.pallas_call(
        kernel,
        in_specs=[SMEM] * scalars + [WHOLE] * (len(operands) - scalars),
        out_specs=out_specs if isinstance(out_shape, list) else out_specs[0],
        out_shape=out_shape,
        scratch_shapes=list(scratch),
        compiler_params=params(mib),
    )(*operands)


def on_device(images, texts, logit_scale, logit_bias):
    rows, width = images.shape
    bf16 = functools.partial(jax.ShapeDtypeStruct, dtype=jnp.bfloat16)
    full = jax.ShapeDtypeStruct((rows, width), jnp.float32)
    half = bf16((rows, width))
    half_pair = bf16((2, rows, width))

    index = lax.axis_index("blk")
    role = jnp.stack([index % 2, index // 2 % CHIPS]).astype(jnp.int32)
    scalars = (role, logit_scale, logit_bias)
    positive = logit_scale[0] > 0

    def together(body, *operands):
        return lax.cond(positive, body, body, *operands)

    partner_images = move(images, partner)
    near = move(texts, near_to)
    guest = move(images, guest_to)
    guest_partner = move(images, guest_partner_to)
    far = move(texts, far_to)
    mine = call(hats_kernel, half_pair, images, partner_images, scalars=0)
    theirs = together(lambda values: move(values, other_core), mine)
    role_type = jax.ShapeDtypeStruct((2,), jnp.int32)
    scalars = (role, logit_scale, logit_bias)
    role, near_hat = call(near_hat_kernel, [role_type, half], role, near, scalars=1, scalar_outs=1)
    scalars = (role, logit_scale, logit_bias)
    slopes_pair = bf16((rows, 2 * rows))
    role, near_grad, mine_slopes, theirs_slopes, back, back_partner, far_grad = call(
        near_kernel,
        [role_type, half, slopes_pair, slopes_pair, half, half, half],
        *scalars, near_hat, mine, theirs, guest, guest_partner, far,
        scratch=[pltpu.VMEM((rows, width), jnp.float32), pltpu.VMEM((2, rows, width), jnp.bfloat16)],
        mib=24,
        scalar_outs=1,
    )
    scalars = (role, logit_scale, logit_bias)
    near_back = move(near_grad, back_to)
    far_back = move(far_grad, far_to, True)
    back_partner = move(back_partner, guest_to, True)
    back = move(back, guest_to, True)
    cross, partner_sum, own_slopes = call(
        sent_kernel,
        [half_pair, full, bf16((rows, 3 * rows))],
        *scalars, texts, mine, theirs, near_hat, mine_slopes, theirs_slopes,
    )

    def sum_with_cross(kernel, slot, dtype, *operands):
        specs = []
        for operand in operands:
            if operand.shape == (2,):
                specs.append(SMEM)
            elif operand.ndim == 3:
                specs.append(pl.BlockSpec((1, rows, width), lambda i: (slot, 0, 0)))
            else:
                specs.append(pl.BlockSpec(operand.shape, lambda i: (0, 0)))
        return pl.pallas_call(
            kernel,
            grid=(1,),
            in_specs=specs,
            out_specs=pl.BlockSpec((rows, width), lambda i: (0, 0)),
            out_shape=jax.ShapeDtypeStruct((rows, width), dtype),
            compiler_params=params(16),
        )(*operands)

    def across(cross, role, partner_sum, back_partner):
        cross = move(cross, other_core)
        return cross, sum_with_cross(partner_kernel, 1, jnp.bfloat16, role, partner_sum, cross, back_partner)

    cross, for_partner = together(across, cross, role, partner_sum, back_partner)
    from_partner = move(for_partner, partner)
    def over(near_back, *kept):
        text_sum, image_sum = call(kept_kernel, [full, full], *kept, mib=20)
        return move(near_back, over_z), text_sum, image_sum

    last_back, text_sum, image_sum = together(
        over, near_back, *scalars, texts, mine, theirs, near_hat, own_slopes, mine_slopes, cross, back
    )
    role, text_grad = call(
        text_final_kernel,
        [jax.ShapeDtypeStruct((2,), jnp.int32), full],
        role, texts, text_sum, near_back, last_back, far_back,
        scalars=1, scalar_outs=1,
    )
    image_grad = call(image_final_kernel, full, role, images, image_sum, from_partner, scalars=1)
    return image_grad, text_grad


def solution(mesh):
    return jax.shard_map(
        on_device,
        mesh=mesh,
        in_specs=(P(AXES, None), P(AXES, None), P(), P()),
        out_specs=(P(AXES, None), P(AXES, None)),
        check_vma=False,
    )
```

```python
import functools

import jax
import jax.numpy as jnp
from jax import lax
from jax.experimental import pallas as pl
from jax.experimental.pallas import tpu as pltpu
from jax.sharding import PartitionSpec as P

AXES = ("blk", "group")
EPSILON = 1e-06
CHIPS = 4

SMEM = pl.BlockSpec(memory_space=pltpu.SMEM)
WHOLE = pl.BlockSpec(memory_space=pltpu.VMEM)


def params(mib):
    return pltpu.CompilerParams(vmem_limit_bytes=mib * 1024 * 1024)


def near_to(b, g, size):
    to = (b + 2) % size
    return to, g ^ (to // (2 * CHIPS) != b // (2 * CHIPS))


def guest_to(b, g, size):
    if b % 2 == 1:
        return None
    return (b - 1 if b // 2 % CHIPS > 0 else b + 2), g


def guest_partner_to(b, g, size):
    return (guest_to(b, g, size)[0], g ^ 1) if b % 2 == 0 else None


def far_to(b, g, size):
    return ((b + 5) % size, g ^ 1) if b % 2 == 1 and b // 2 % CHIPS == CHIPS - 2 else None


def back_to(b, g, size):
    to = (b - 2) % size
    if to // (2 * CHIPS) == b // (2 * CHIPS):
        return to, g
    return (to, g ^ 1) if b % 2 == 0 else (b + 2 * CHIPS - 2, g)


def over_z(b, g, size):
    return ((b + 2 * CHIPS) % size, g ^ 1) if b % 2 == 1 and b // 2 % CHIPS == CHIPS - 1 else None


def other_core(b, g, size):
    return b ^ 1, g


def partner(b, g, size):
    return b, g ^ 1


def move(values, where, inverse=False):
    n_blk, n_group = lax.axis_size("blk"), lax.axis_size("group")
    pairs = []
    for b in range(n_blk):
        for g in range(n_group):
            to = where(b, g, n_blk)
            if to is not None:
                pair = (b * n_group + g, to[0] * n_group + to[1])
                pairs.append(pair[::-1] if inverse else pair)
    return lax.ppermute(values, AXES, sorted(pairs))


def normalize(values):
    full = values.astype(jnp.float32)
    inverse = lax.rsqrt(jnp.sum(full * full, axis=-1, keepdims=True) + EPSILON)
    return full * inverse, inverse


def hat(values):
    return normalize(values)[0].astype(jnp.bfloat16)


def dot(left, right, left_dim, right_dim):
    return lax.dot_general(
        left, right, (((left_dim,), (right_dim,)), ((), ())), preferred_element_type=jnp.float32
    )


def slopes_of(text_hat, image_hat, scale, bias, same=None):
    half = 0.5 * scale
    slopes = half * jnp.tanh(half * dot(text_hat, image_hat, 1, 1) + 0.5 * bias) + half
    if same is not None:
        slopes = slopes - scale * same
    return slopes.astype(jnp.bfloat16)


def rows_of(ref):
    count, rows, width = ref.shape
    return ref[...].reshape(count * rows, width)


def is_odd(role):
    return role[0] == 1


def has_guests(role):
    return jnp.logical_and(role[0] == 1, role[1] < CHIPS - 1)


def takes_far(role):
    return jnp.logical_and(role[0] == 0, role[1] == 1)


def pass_on(role, role_out):
    role_out[0] = role[0]
    role_out[1] = role[1]


def near_hat_kernel(role, text_ref, role_out, hat_ref):
    pass_on(role, role_out)
    hat_ref[...] = hat(text_ref[...])


def hats_kernel(image_ref, partner_ref, hats_ref):
    hats_ref[0] = hat(image_ref[...])
    hats_ref[1] = hat(partner_ref[...])


def near_kernel(
    role, scale_ref, bias_ref, hat_ref, mine_ref, theirs_ref, guest_ref, guest_partner_ref, far_ref,
    role_out, grad_ref, mine_slopes_ref, theirs_slopes_ref, back_ref, back_partner_ref, far_grad_ref,
    total, guests_ref,
):
    pass_on(role, role_out)
    scale, bias = scale_ref[0], bias_ref[0]
    rows, width = hat_ref.shape
    near_hat = hat_ref[...]
    mine, theirs = rows_of(mine_ref), rows_of(theirs_ref)
    mine_slopes = slopes_of(near_hat, mine, scale, bias)
    mine_slopes_ref[...] = mine_slopes
    theirs_slopes = slopes_of(near_hat, theirs, scale, bias)
    theirs_slopes_ref[...] = theirs_slopes
    total[...] = dot(mine_slopes, mine, 1, 0) + dot(theirs_slopes, theirs, 1, 0)

    def visits(text_hat):
        guests_ref[0] = hat(guest_ref[...])
        guests_ref[1] = hat(guest_partner_ref[...])
        guests = rows_of(guests_ref)
        slopes = slopes_of(text_hat, guests, scale, bias)
        back_ref[...] = dot(slopes[:, :rows], text_hat, 0, 0).astype(back_ref.dtype)
        back_partner_ref[...] = dot(slopes[:, rows:], text_hat, 0, 0).astype(back_partner_ref.dtype)
        return slopes, guests

    @pl.when(has_guests(role))
    def _():
        slopes, guests = visits(hat_ref[...])
        total[...] += dot(slopes, guests, 1, 0)

    @pl.when(takes_far(role))
    def _():
        slopes, guests = visits(hat(far_ref[...]))
        far_grad_ref[...] = dot(slopes, guests, 1, 0).astype(far_grad_ref.dtype)

    grad_ref[...] = total[...].astype(grad_ref.dtype)


def sent_kernel(
    role, scale_ref, bias_ref, text_ref, mine_ref, theirs_ref, hat_ref, mine_slopes_ref, theirs_slopes_ref,
    cross_ref, partner_sum_ref, slopes_ref,
):
    scale, bias = scale_ref[0], bias_ref[0]
    rows, width = text_ref.shape
    text_hat = hat(text_ref[...])
    slopes = slopes_of(text_hat, mine_ref[1], scale, bias)
    slopes_ref[:, :rows] = slopes
    total = dot(slopes, text_hat, 0, 0) + dot(mine_slopes_ref[:, rows:], hat_ref[...], 0, 0)
    partner_sum_ref[...] = total.astype(partner_sum_ref.dtype)

    @pl.when(role[0] == 0)
    def _():
        text_hat = hat(text_ref[...])
        slopes = slopes_of(text_hat, rows_of(theirs_ref), scale, bias)
        slopes_ref[:, rows:] = slopes
        for slot in range(2):
            at = slice(slot * rows, (slot + 1) * rows)
            total = dot(theirs_slopes_ref[:, at], hat_ref[...], 0, 0) + dot(slopes[:, at], text_hat, 0, 0)
            cross_ref[slot] = total.astype(cross_ref.dtype)

    @pl.when(role[0] == 1)
    def _():
        for slot in range(2):
            at = slice(slot * rows, (slot + 1) * rows)
            cross_ref[slot] = dot(theirs_slopes_ref[:, at], hat_ref[...], 0, 0).astype(cross_ref.dtype)


def kept_kernel(
    role, scale_ref, bias_ref, text_ref, mine_ref, theirs_ref, hat_ref, slopes_ref, mine_slopes_ref, cross_ref, back_ref,
    text_sum_ref, image_sum_ref,
):
    scale, bias = scale_ref[0], bias_ref[0]
    rows, width = hat_ref.shape
    text_hat = hat(text_ref[...])
    same = (
        lax.broadcasted_iota(jnp.int32, (rows, rows), 0) == lax.broadcasted_iota(jnp.int32, (rows, rows), 1)
    ).astype(jnp.float32)
    slopes = slopes_of(text_hat, mine_ref[0], scale, bias, same)
    even = 1.0 - is_odd(role).astype(jnp.float32)
    image_sum_ref[...] = (
        dot(slopes, text_hat, 0, 0)
        + dot(mine_slopes_ref[:, :rows], hat_ref[...], 0, 0)
        + cross_ref[0].astype(jnp.float32)
        + even * back_ref[...].astype(jnp.float32)
    )
    text_sum_ref[...] = dot(slopes, mine_ref[0], 1, 0) + dot(slopes_ref[:, :rows], mine_ref[1], 1, 0)

    @pl.when(role[0] == 0)
    def _():
        text_sum_ref[...] += dot(slopes_ref[:, rows:], rows_of(theirs_ref), 1, 0)


def partner_kernel(role, sum_ref, cross_ref, back_ref, out_ref):
    even = 1.0 - is_odd(role).astype(jnp.float32)
    total = sum_ref[...].astype(jnp.float32) + cross_ref[0].astype(jnp.float32) + even * back_ref[...].astype(jnp.float32)
    out_ref[...] = total.astype(out_ref.dtype)


def project(raw, total):
    unit, inverse = normalize(raw)
    return (total - unit * jnp.sum(unit * total, axis=-1, keepdims=True)) * inverse


def text_final_kernel(role, texts, text_sum, near_back, last_back, far_back, role_out, out_ref):
    pass_on(role, role_out)
    last = jnp.logical_and(role[0] == 1, role[1] == CHIPS - 1)
    near = jnp.where(last, last_back[...].astype(jnp.float32), near_back[...].astype(jnp.float32))
    total = text_sum[...] + near + far_back[...].astype(jnp.float32)
    out_ref[...] = project(texts[...], total)


def image_final_kernel(role, images, image_sum, from_partner, out_ref):
    total = image_sum[...] + from_partner[...].astype(jnp.float32)
    out_ref[...] = project(images[...], total)


def call(kernel, out_shape, *operands, mib=16, scalars=3, scalar_outs=0, scratch=()):
    outs = out_shape if isinstance(out_shape, list) else [out_shape]
    out_specs = [SMEM] * scalar_outs + [WHOLE] * (len(outs) - scalar_outs)
    return pl.pallas_call(
        kernel,
        in_specs=[SMEM] * scalars + [WHOLE] * (len(operands) - scalars),
        out_specs=out_specs if isinstance(out_shape, list) else out_specs[0],
        out_shape=out_shape,
        scratch_shapes=list(scratch),
        compiler_params=params(mib),
    )(*operands)


def on_device(images, texts, logit_scale, logit_bias):
    rows, width = images.shape
    bf16 = functools.partial(jax.ShapeDtypeStruct, dtype=jnp.bfloat16)
    full = jax.ShapeDtypeStruct((rows, width), jnp.float32)
    half = bf16((rows, width))
    half_pair = bf16((2, rows, width))

    index = lax.axis_index("blk")
    role = jnp.stack([index % 2, index // 2 % CHIPS]).astype(jnp.int32)
    scalars = (role, logit_scale, logit_bias)
    positive = logit_scale[0] > 0

    def together(body, *operands):
        return lax.cond(positive, body, body, *operands)

    partner_images = move(images, partner)
    near = move(texts, near_to)
    guest = move(images, guest_to)
    guest_partner = move(images, guest_partner_to)
    far = move(texts, far_to)
    mine = call(hats_kernel, half_pair, images, partner_images, scalars=0)
    theirs = together(lambda values: move(values, other_core), mine)
    role_type = jax.ShapeDtypeStruct((2,), jnp.int32)
    scalars = (role, logit_scale, logit_bias)
    role, near_hat = call(near_hat_kernel, [role_type, half], role, near, scalars=1, scalar_outs=1)
    scalars = (role, logit_scale, logit_bias)
    slopes_pair = bf16((rows, 2 * rows))
    role, near_grad, mine_slopes, theirs_slopes, back, back_partner, far_grad = call(
        near_kernel,
        [role_type, half, slopes_pair, slopes_pair, half, half, half],
        *scalars, near_hat, mine, theirs, guest, guest_partner, far,
        scratch=[pltpu.VMEM((rows, width), jnp.float32), pltpu.VMEM((2, rows, width), jnp.bfloat16)],
        mib=24,
        scalar_outs=1,
    )
    scalars = (role, logit_scale, logit_bias)
    near_back = move(near_grad, back_to)
    far_back = move(far_grad, far_to, True)
    back_partner = move(back_partner, guest_to, True)
    back = move(back, guest_to, True)
    cross, partner_sum, own_slopes = call(
        sent_kernel,
        [half_pair, half, bf16((rows, 3 * rows))],
        *scalars, texts, mine, theirs, near_hat, mine_slopes, theirs_slopes,
    )

    def sum_with_cross(kernel, slot, dtype, *operands):
        specs = []
        for operand in operands:
            if operand.shape == (2,):
                specs.append(SMEM)
            elif operand.ndim == 3:
                specs.append(pl.BlockSpec((1, rows, width), lambda i: (slot, 0, 0)))
            else:
                specs.append(pl.BlockSpec(operand.shape, lambda i: (0, 0)))
        return pl.pallas_call(
            kernel,
            grid=(1,),
            in_specs=specs,
            out_specs=pl.BlockSpec((rows, width), lambda i: (0, 0)),
            out_shape=jax.ShapeDtypeStruct((rows, width), dtype),
            compiler_params=params(16),
        )(*operands)

    def across(cross, role, partner_sum, back_partner):
        cross = move(cross, other_core)
        return cross, sum_with_cross(partner_kernel, 1, jnp.bfloat16, role, partner_sum, cross, back_partner)

    cross, for_partner = together(across, cross, role, partner_sum, back_partner)
    from_partner = move(for_partner, partner)
    def over(near_back, *kept):
        text_sum, image_sum = call(kept_kernel, [full, full], *kept, mib=20)
        return move(near_back, over_z), text_sum, image_sum

    last_back, text_sum, image_sum = together(
        over, near_back, *scalars, texts, mine, theirs, near_hat, own_slopes, mine_slopes, cross, back
    )
    role, text_grad = call(
        text_final_kernel,
        [jax.ShapeDtypeStruct((2,), jnp.int32), full],
        role, texts, text_sum, near_back, last_back, far_back,
        scalars=1, scalar_outs=1,
    )
    image_grad = call(image_final_kernel, full, role, images, image_sum, from_partner, scalars=1)
    return image_grad, text_grad


def solution(mesh):
    return jax.shard_map(
        on_device,
        mesh=mesh,
        in_specs=(P(AXES, None), P(AXES, None), P(), P()),
        out_specs=(P(AXES, None), P(AXES, None)),
        check_vma=False,
    )
```
